128 devices in a mesh: seq: 4 (over x_hi, core), wide: 32 (over z, y, x_lo).
Axes of the slice: x: 4 (x_hi: 2, x_lo: 2; x = x_hi * 2 + x_lo), y: 4, z: 4, core: 2. Of those that a mesh axis runs over, the one named last changes fastest.
Arguments:
- frames: bfloat16 [32, 512, 1536], P('wide', 'seq'), may hold values from -6 to 6
- cotangent: bfloat16 [32, 512, 1536], P('wide', 'seq'), may hold values from -6 to 6
- gain_in: float32 [1536], replicated, may hold values from 0.5 to 1.5
- w_in: bfloat16 [1536, 3072], P('wide'), may hold values from -0.15625 to 0.15625
- kernel: float32 [31, 1536], replicated, may hold values from -1 to 1
- gain_mid: float32 [1536], replicated, may hold values from 0.5 to 1.5
- w_out: bfloat16 [1536, 1536], P('wide'), may hold values from -0.15625 to 0.15625
- group_len: int32 [32, 4], P('wide', 'seq'), may hold values from 64 to 128, as said below
- starts: int32 [32, 16], P('wide', 'seq'), may hold values from 0 to 128, as said below
Outputs:
- outputs: bfloat16 [32, 512, 1536], P('wide', 'seq')
- grad_frames: bfloat16 [32, 512, 1536], P('wide', 'seq')
- grad_w_in: float32 [1536, 3072], P('wide')
- grad_w_out: float32 [1536, 1536], P('wide')
- grad_kernel: float32 [31, 1536], replicated
- grad_gain_in: float32 [1536], replicated
- grad_gain_mid: float32 [1536], replicated
The draws below stay inside these ranges and needn't reach their ends.
Inputs may be any that keep to these rules, and one draw needn't show every extreme that they name: `group_len`: some group has length exactly 128. Each group has 4 slots; a slot holds an offset below the group's length where an utterance starts, or 128 when unused. Slots are in no order and may repeat.
All inputs are finite; a program needn't handle non-finite values.
Results may differ from the reference program's by a relative error of at most 0.025.
Values may be sent and summed in bfloat16 or wider, within the bound.
No kernel may reach another device: no remote copies, remote signals or barrier semaphores. Data moves between devices by JAX's collectives and lax.ppermute only.
A program may use at most 128 MiB of HBM per device.

```python
import jax
import jax.numpy as jnp
from jax import lax

D = 1536
KW = 31
HALF = 15
NB = 4
TOK_DEV = 128
STREAMS = 32
FRAMES = 512
N_SEQ = 4


def group_plan(key):
    groups = FRAMES // TOK_DEV
    first, second = jax.random.split(jax.random.fold_in(key, 7))
    cut = jax.random.randint(first, (STREAMS, groups), 0, TOK_DEV // 2 + 1)
    full_at = jax.random.randint(second, (), 0, STREAMS * groups)
    where_full = jnp.arange(STREAMS * groups).reshape(STREAMS, groups) == full_at
    cut = jnp.where(where_full, 0, cut)
    return (TOK_DEV - cut).astype(jnp.int32)


def draw_group_len(key, part):
    return group_plan(key)


def draw_starts(key, part):
    groups = FRAMES // TOK_DEV
    lengths = group_plan(key)
    third, fourth = jax.random.split(jax.random.fold_in(key, 11))
    offset = jax.random.randint(third, (STREAMS, groups, NB), 0, TOK_DEV)
    offset = offset % lengths[:, :, None]
    used = jax.random.randint(fourth, (STREAMS, groups, NB), 0, 2)
    return jnp.where(used == 1, offset, TOK_DEV).reshape(STREAMS, groups * NB).astype(jnp.int32)


def levels(rng, dims, cuts, low, high):
    def one(axis_at, shards_of):
        heights = jax.random.uniform(jax.random.fold_in(jax.random.fold_in(rng, 6), axis_at), (shards_of,), jnp.float32, low / len(cuts), high / len(cuts))
        return jnp.repeat(jnp.exp(heights), dims[axis_at] // shards_of).reshape((-1,) + (1,) * (len(dims) - axis_at - 1))

    loudness = one(*cuts[0])
    for cut in cuts[1:]:
        loudness = loudness * one(*cut)
    return loudness


def gaussian(key, shape, scale, reach, shards=(), kind=jnp.bfloat16):
    loudness = levels(key, shape, shards, -0.22, 0.18) if shards else 1.0
    result = jax.random.normal(key, shape, jnp.float32) * scale * loudness
    return jnp.minimum(jnp.maximum(result, -reach), reach).astype(kind)


def setup_inputs(seed: int = 0) -> dict:
    key_list = jax.random.split(jax.random.key(seed), 10)
    return {
        "frames": gaussian(key_list[0], (STREAMS, FRAMES, D), 1.0, 6.0, ((0, 32), (1, 4))),
        "cotangent": gaussian(key_list[1], (STREAMS, FRAMES, D), 1.0, 6.0, ((0, 32), (1, 4))),
        "gain_in": jnp.clip(1.0 + 0.1 * jax.random.normal(key_list[2], (D,), jnp.float32), 0.5, 1.5),
        "w_in": gaussian(key_list[3], (D, 2 * D), D ** -0.5, 0.15625, ((0, 32),)),
        "kernel": gaussian(key_list[4], (KW, D), KW ** -0.5, 1.0, (), jnp.float32),
        "gain_mid": jnp.clip(1.0 + 0.1 * jax.random.normal(key_list[5], (D,), jnp.float32), 0.5, 1.5),
        "w_out": gaussian(key_list[6], (D, D), D ** -0.5, 0.15625, ((0, 32),)),
        "group_len": draw_group_len(jax.random.fold_in(key_list[9], 71), 0),
        "starts": draw_starts(jax.random.fold_in(key_list[9], 71), 0),
    }


EPS = 1e-05

def layer_norm(values):
    mean = lax.optimization_barrier(jnp.mean(values, -1, keepdims=True))
    centred = values - mean
    inverse = lax.rsqrt(lax.optimization_barrier(jnp.mean(centred * centred, -1, keepdims=True)) + EPS)
    return (centred * inverse, inverse)

def norm_back(grad, normed, inverse):
    return inverse * (grad - lax.optimization_barrier(jnp.mean(grad, -1, keepdims=True)) - normed * lax.optimization_barrier(jnp.mean(grad * normed, -1, keepdims=True)))

def group_labels(bounds, length):
    places = jnp.arange(TOK_DEV, dtype=jnp.int32)
    labels = lax.optimization_barrier(jnp.sum((bounds[:, None] <= places[None, :]).astype(jnp.int32), 0))
    last = jnp.sum((bounds <= length - 1).astype(jnp.int32))
    return (labels, last, places < length)

def front(frames, gain_in, w_in, validf):
    normed, inverse = layer_norm(frames.astype(jnp.float32))
    act = (normed * gain_in).astype(jnp.bfloat16)
    hidden = jnp.dot(act, w_in, preferred_element_type=jnp.float32)
    width = hidden.shape[1] // 2
    gated = (hidden[:, :width] * jax.nn.sigmoid(hidden[:, width:]) * validf[:, None]).astype(jnp.bfloat16)
    return (normed, inverse, act, hidden, gated)

def outer_rims(gated, labels, last, length):
    begin = (length - HALF).astype(jnp.int32)
    tail = lax.dynamic_slice_in_dim(gated, begin, HALF, 0)
    tail_labels = lax.dynamic_slice_in_dim(labels, begin, HALF, 0)
    tail_flag = (tail_labels == last).astype(jnp.bfloat16)
    head = gated[:HALF]
    head_flag = (labels[:HALF] == 0).astype(jnp.bfloat16)
    return (tail, tail_flag, head, head_flag)

def extend(gated, labels, last, valid, length, left, left_flag, right, right_flag):
    rows = gated.shape[0]
    place = (length + HALF).astype(jnp.int32)
    ext = jnp.concatenate([left, gated, jnp.zeros((HALF, gated.shape[1]), jnp.bfloat16)], 0)
    ext = lax.dynamic_update_slice_in_dim(ext, right, place, 0)
    mine = jnp.where(valid, labels, -3).astype(jnp.int32)
    left_ids = jnp.where(left_flag > 0.5, 0, -1).astype(jnp.int32)
    right_ids = jnp.where(right_flag > 0.5, last, -2).astype(jnp.int32)
    ids = jnp.concatenate([left_ids, mine, jnp.full((HALF,), -3, jnp.int32)])
    ids = lax.dynamic_update_slice_in_dim(ids, right_ids, place, 0)
    taps = jnp.stack([(ids[k:k + rows] == labels) & valid for k in range(KW)]).astype(jnp.float32)
    return (ext, taps)

def depthwise(ext, taps, kernel):
    rows = taps.shape[1]
    total = jnp.zeros((rows, ext.shape[1]), jnp.float32)
    for k in range(KW):
        total = total + kernel[k] * taps[k][:, None] * ext[k:k + rows].astype(jnp.float32)
    return total

def depthwise_back(ext, taps, kernel, grad):
    rows = taps.shape[1]
    dext = jnp.zeros((rows + 2 * HALF, grad.shape[1]), jnp.float32)
    dker = []
    for k in range(KW):
        masked = taps[k][:, None] * grad
        dker.append(lax.optimization_barrier(jnp.sum(masked * ext[k:k + rows].astype(jnp.float32), 0)))
        dext = dext.at[k:k + rows].add(kernel[k] * masked)
    return (dext, jnp.stack(dker))

def middle(ext, taps, kernel, gain_mid, w_out, frames, validf):
    conv = depthwise(ext, taps, kernel)
    normed_mid, inverse_mid = layer_norm(conv)
    scaled = normed_mid * gain_mid
    swished = (scaled * jax.nn.sigmoid(scaled)).astype(jnp.bfloat16)
    proj = jnp.dot(swished, w_out, preferred_element_type=jnp.float32)
    outputs = ((frames.astype(jnp.float32) + proj) * validf[:, None]).astype(jnp.bfloat16)
    return (normed_mid, inverse_mid, scaled, swished, outputs)

def back_mid(cotangent, validf, scaled, normed_mid, inverse_mid, gain_mid, w_out):
    grad_y = (cotangent.astype(jnp.float32) * validf[:, None]).astype(jnp.bfloat16)
    dswished = lax.dot_general(grad_y, w_out, (((1,), (1,)), ((), ())), preferred_element_type=jnp.float32)
    sig = jax.nn.sigmoid(scaled)
    dscaled = dswished * sig * (1.0 + scaled * (1.0 - sig))
    dgain_mid = lax.optimization_barrier(jnp.sum(dscaled * normed_mid, 0))
    dconv = norm_back(dscaled * gain_mid, normed_mid, inverse_mid)
    return (grad_y, dconv, dgain_mid)

def collect_grad(dext, from_next, from_prev, length, validf):
    rows = validf.shape[0]
    own = dext[HALF:HALF + rows]
    own = own + lax.dynamic_update_slice_in_dim(jnp.zeros_like(own), from_next, (length - HALF).astype(jnp.int32), 0)
    own = own + jnp.pad(from_prev, ((0, rows - HALF), (0, 0)))
    return own * validf[:, None]

def back_front(dgated, hidden, normed, inverse, gain_in, w_in, grad_y, validf):
    width = hidden.shape[1] // 2
    first = hidden[:, :width]
    sig = jax.nn.sigmoid(hidden[:, width:])
    dhidden = jnp.concatenate([dgated * sig, dgated * first * sig * (1.0 - sig)], 1).astype(jnp.bfloat16)
    dact = lax.dot_general(dhidden, w_in, (((1,), (1,)), ((), ())), preferred_element_type=jnp.float32)
    dgain_in = lax.optimization_barrier(jnp.sum(dact * normed, 0))
    grad_frames = ((grad_y.astype(jnp.float32) + norm_back(dact * gain_in, normed, inverse)) * validf[:, None]).astype(jnp.bfloat16)
    return (dhidden, dgain_in, grad_frames)

def column_product(left, right):
    return lax.dot_general(left, right, (((0,), (0,)), ((), ())), preferred_element_type=jnp.float32)

def from_prev(values):
    return jnp.concatenate([jnp.zeros_like(values[:1]), values[:-1]], 0)

def from_next(values):
    return jnp.concatenate([values[1:], jnp.zeros_like(values[:1])], 0)

def reference(frames, cotangent, gain_in, w_in, kernel, gain_mid, w_out, group_len, starts):
    bounds = starts.reshape(STREAMS, N_SEQ, NB)

    def one_stream(carry, item):
        acc_in, acc_out, acc_kernel, acc_gin, acc_gmid = carry
        stream_frames, stream_cot, lengths, stream_bounds = item
        xs = stream_frames.reshape(N_SEQ, TOK_DEV, D)
        cots = stream_cot.reshape(N_SEQ, TOK_DEV, D)
        labels, last, valid = jax.vmap(group_labels)(stream_bounds, lengths)
        validf = valid.astype(jnp.float32)
        normed, inverse, act, hidden, gated = jax.vmap(front, in_axes=(0, None, None, 0))(xs, gain_in, w_in, validf)
        tail, tail_flag, head, head_flag = jax.vmap(outer_rims)(gated, labels, last, lengths)
        ext, taps = jax.vmap(extend)(gated, labels, last, valid, lengths, from_prev(tail), from_prev(tail_flag), from_next(head), from_next(head_flag))
        normed_mid, inverse_mid, scaled, swished, outputs = jax.vmap(middle, in_axes=(0, 0, None, None, None, 0, 0))(ext, taps, kernel, gain_mid, w_out, xs, validf)
        grad_y, dconv, dgain_mid = jax.vmap(back_mid, in_axes=(0, 0, 0, 0, 0, None, None))(cots, validf, scaled, normed_mid, inverse_mid, gain_mid, w_out)
        dext, dker = jax.vmap(depthwise_back, in_axes=(0, 0, None, 0))(ext, taps, kernel, dconv)
        left_grads = dext[:, :HALF]
        right_grads = jax.vmap(lambda block, length: lax.dynamic_slice_in_dim(block, (length + HALF).astype(jnp.int32), HALF, 0))(dext, lengths)
        dgated = jax.vmap(collect_grad)(dext, from_next(left_grads), from_prev(right_grads), lengths, validf)
        dhidden, dgain_in, grad_frames = jax.vmap(back_front, in_axes=(0, 0, 0, 0, None, None, 0, 0))(dgated, hidden, normed, inverse, gain_in, w_in, grad_y, validf)
        terms_in = jax.vmap(column_product)(act, dhidden).astype(jnp.bfloat16).astype(jnp.float32)
        terms_out = jax.vmap(column_product)(swished, grad_y).astype(jnp.bfloat16).astype(jnp.float32)
        carry = (acc_in + lax.optimization_barrier(jnp.sum(terms_in, 0)), acc_out + lax.optimization_barrier(jnp.sum(terms_out, 0)), acc_kernel + lax.optimization_barrier(jnp.sum(dker, 0)), acc_gin + lax.optimization_barrier(jnp.sum(dgain_in, 0)), acc_gmid + lax.optimization_barrier(jnp.sum(dgain_mid, 0)))
        return (carry, (outputs.reshape(FRAMES, D), grad_frames.reshape(FRAMES, D)))
    start = (jnp.zeros((D, 2 * D), jnp.float32), jnp.zeros((D, D), jnp.float32), jnp.zeros((KW, D), jnp.float32), jnp.zeros((D,), jnp.float32), jnp.zeros((D,), jnp.float32))
    carry, stacked = lax.scan(one_stream, start, (frames, cotangent, group_len, bounds))
    return (stacked[0], stacked[1], carry[0], carry[1], carry[2], carry[3], carry[4])
```

```python
import jax
import jax.numpy as jnp
from jax import lax
from jax.sharding import PartitionSpec as P

EPS = 1e-05
N_SEQ = 4
NZ, NY, NX = 4, 4, 2
GAP = 16
SPREAD = 768
bf16 = jnp.bfloat16
f32 = jnp.float32


def wide_index(z, y, x):
    return (z * NY + y) * NX + x


def by_xor(axis, d):
    pairs = []
    for z in range(NZ):
        for y in range(NY):
            for x in range(NX):
                to = {"z": (z ^ d, y, x), "y": (z, y ^ d, x), "x": (z, y, x ^ d)}[axis]
                pairs.append((wide_index(z, y, x), wide_index(*to)))
    return pairs


def swap_wide(value, axis, d):
    return lax.ppermute(value, "wide", by_xor(axis, d))


def swap_seq(value, d):
    return lax.ppermute(value, "seq", [(i, i ^ d) for i in range(N_SEQ)])


def swap_z_seq(value):
    pairs = []
    for s in range(N_SEQ):
        for z in range(NZ):
            for y in range(NY):
                for x in range(NX):
                    pairs.append(
                        (s * 32 + wide_index(z, y, x), z * 32 + wide_index(s, y, x))
                    )
    return lax.ppermute(value, ("seq", "wide"), pairs)


def in_order(pieces, me):
    count = len(pieces)
    d = 1
    while d < count:
        odd = (me & d) != 0
        pieces = [jnp.where(odd, pieces[j ^ d], pieces[j]) for j in range(count)]
        d *= 2
    return pieces


def gather4(value, axis):
    return [value] + [swap_wide(value, axis, d) for d in (1, 2, 3)]


def gather_seq(value):
    core = swap_seq(value, 1)
    far = swap_seq(value, 2)
    return [value, core, far, swap_seq(far, 1)]


def scatter_seq(parts):
    sent = swap_seq(jnp.stack([parts[1], parts[3]]).astype(bf16), 1).astype(f32)
    far = swap_seq((parts[2] + sent[1]).astype(bf16), 2).astype(f32)
    return parts[0] + sent[0] + far


def scatter4(block, me, axis):
    total = block(me).astype(f32)
    for d in (1, 3, 2):
        total = total + swap_wide(block(me ^ d).astype(bf16), axis, d).astype(f32)
    return total


def scatter2(block, me):
    return block(me).astype(f32) + swap_wide(block(me ^ 1).astype(bf16), "x", 1).astype(f32)


def layer_norm(values):
    mean = jnp.mean(values, -1, keepdims=True)
    centred = values - mean
    inverse = lax.rsqrt(jnp.mean(centred * centred, -1, keepdims=True) + EPS)
    return (centred * inverse, inverse)


def norm_back(grad, normed, inverse):
    return inverse * (
        grad
        - jnp.mean(grad, -1, keepdims=True)
        - normed * jnp.mean(grad * normed, -1, keepdims=True)
    )


def two_terms(x):
    high = lax.reduce_precision(x, 8, 7)
    return jnp.concatenate([high.astype(bf16), (x - high).astype(bf16)], 1)


def moved(one_hot, x):
    both = jnp.dot(one_hot, two_terms(x), preferred_element_type=f32)
    width = x.shape[1]
    return both[:, :width] + both[:, width:]


def column_product(left, right):
    return lax.dot_general(left, right, (((0,), (0,)), ((), ())), preferred_element_type=f32)


def row_product(left, right):
    return lax.dot_general(left, right, (((1,), (1,)), ((), ())), preferred_element_type=f32)


def shards(frames, cotangent, gain_in, w_in, kernel, gain_mid, w_out, group_len, starts):
    taps_count = kernel.shape[0]
    half = (taps_count - 1) // 2
    xs = frames[0]
    rows, width = xs.shape
    part = width // N_SEQ
    s = lax.axis_index("seq")
    wide = lax.axis_index("wide")
    z, y, x = wide // (NY * NX), (wide // NX) % NY, wide % NX
    mine = s * part
    length = group_len[0, 0]
    validf = (jnp.arange(rows, dtype=jnp.int32) < length).astype(f32)[:, None]

    wa = lax.dynamic_slice_in_dim(w_in, mine, part, 1)
    wb = lax.dynamic_slice_in_dim(w_in, width + mine, part, 1)
    wab = jnp.stack([wa, wb])
    wab = jnp.concatenate(in_order([wab, swap_wide(wab, "x", 1)], x), 1)
    wa = jnp.concatenate(in_order(gather4(wab[0], "y"), y), 0)
    wb = jnp.stack(in_order(gather4(wab[1], "z"), z), 0)
    wa = jnp.concatenate(in_order(gather4(wa, "z"), z), 0)
    wb = jnp.stack(in_order(gather4(wb, "y"), y), 1).reshape(width, part)
    wo = swap_z_seq(w_out)
    wo = jnp.concatenate(in_order([wo, swap_wide(wo, "x", 1)], x), 0)
    wo = jnp.concatenate(in_order(gather4(wo, "y"), y), 0)

    normed, inverse = layer_norm(xs.astype(f32))
    own_act = (normed * gain_in).astype(bf16)
    own_gy = (cotangent[0].astype(f32) * validf).astype(bf16)
    act = jnp.concatenate(gather_seq(own_act), 0)
    grad_y = jnp.concatenate(gather_seq(own_gy), 0)

    meta = lax.all_gather(jnp.concatenate([group_len[0], starts[0]]), "seq")
    lens, bounds = meta[:, 0], meta[:, 1:]
    used_starts = jnp.sum((bounds < lens[:, None]).astype(jnp.int32), 1)
    offset = lens + GAP * used_starts
    place = []
    o = jnp.arange(rows, dtype=jnp.int32)
    groups = jnp.arange(N_SEQ, dtype=jnp.int32)
    for j in range(N_SEQ):
        g = s ^ j
        pick = (groups == g).astype(jnp.int32)
        base = jnp.sum(jnp.where(groups < g, offset, 0))
        glen = jnp.sum(pick * lens)
        gbounds = jnp.sum(pick[:, None] * bounds, 0)
        label = jnp.sum((gbounds[:, None] <= o[None, :]).astype(jnp.int32), 0)
        place.append(jnp.where(o < glen, base + o + GAP * label, -1))
    place = jnp.concatenate(place)
    spots = jnp.arange(SPREAD, dtype=jnp.int32)
    spread = (spots[:, None] == place[None, :]).astype(bf16)
    back = (place[:, None] == spots[None, :]).astype(bf16)

    hidden_a = jnp.dot(act, wa, preferred_element_type=f32)
    hidden_b = jnp.dot(act, wb, preferred_element_type=f32)
    sig_gate = jax.nn.sigmoid(hidden_b)
    gated = (hidden_a * sig_gate).astype(bf16)
    gated = jnp.dot(spread, gated, preferred_element_type=f32)
    padded = jnp.pad(gated, ((half, half), (0, 0)))
    taps = lax.dynamic_slice_in_dim(kernel, mine, part, 1)
    gain = lax.dynamic_slice_in_dim(gain_mid, mine, part, 0)
    conv = taps[0] * padded[:SPREAD]
    for k in range(1, taps_count):
        conv = conv + taps[k] * padded[k : k + SPREAD]

    mean = jnp.mean(conv, 1)
    square = jnp.sum((conv - mean[:, None]) ** 2, 1)
    stats = jnp.stack([mean, square])
    stats = jnp.stack([stats] + [swap_seq(stats, d) for d in (1, 2, 3)])
    mean = jnp.mean(stats[:, 0], 0)
    square = jnp.sum(stats[:, 1], 0) + part * jnp.sum((stats[:, 0] - mean) ** 2, 0)
    inverse_mid = lax.rsqrt(square / width + EPS)[:, None]
    normed_mid = (conv - mean[:, None]) * inverse_mid
    scaled = normed_mid * gain
    sig_mid = jax.nn.sigmoid(scaled)
    swished = jnp.dot(
        back, (scaled * sig_mid).astype(bf16), preferred_element_type=f32
    ).astype(bf16)

    dswished = moved(spread, row_product(grad_y, wo))
    dscaled = dswished * sig_mid * (1.0 + scaled * (1.0 - sig_mid))
    dgain_mid = jnp.sum(dscaled * normed_mid, 0)
    grad = dscaled * gain
    stats = jnp.stack([jnp.sum(grad, 1), jnp.sum(grad * normed_mid, 1)])
    stats = stats + swap_seq(stats, 1) + swap_seq(stats, 2) + swap_seq(stats, 3)
    stats = stats / width
    dconv = inverse_mid * (grad - stats[0][:, None] - normed_mid * stats[1][:, None])

    def rows_out(i):
        return column_product(
            lax.dynamic_slice_in_dim(swished, i * (part // NY), part // NY, 1), grad_y
        ).astype(bf16)

    dwo = column_product(swished, grad_y).astype(bf16)
    block = part // NY
    dwo = scatter4(lambda i: lax.dynamic_slice_in_dim(dwo, i * block, block, 0), y, "y")
    dwo2 = dwo.astype(bf16)
    dwo = scatter2(lambda i: lax.dynamic_slice_in_dim(dwo2, i * (block // 2), block // 2, 0), x)
    dwo3 = dwo.astype(bf16)
    dwo = scatter4(lambda i: lax.dynamic_slice_in_dim(dwo3, i * part, part, 1), z, "z")
    dwo = swap_z_seq(dwo.astype(bf16))

    padded_back = jnp.pad(dconv, ((half, half), (0, 0)))
    dgated = taps[0] * padded_back[2 * half : 2 * half + SPREAD]
    for k in range(1, taps_count):
        dgated = dgated + taps[k] * padded_back[2 * half - k : 2 * half - k + SPREAD]
    dker = jnp.stack(
        [jnp.sum(dconv * padded[k : k + SPREAD], 0) for k in range(taps_count)]
    )
    dgated = moved(back, dgated)
    da = (dgated * sig_gate).astype(bf16)
    db = (dgated * hidden_a * sig_gate * (1.0 - sig_gate)).astype(bf16)

    dwa = column_product(act, da).astype(bf16).reshape(NZ, width // NZ, part)
    dwb = column_product(act, db).astype(bf16).reshape(NZ, NY, width // NZ // NY, part)
    dwa = scatter4(lambda i: lax.dynamic_index_in_dim(dwa, i, 0, False), z, "z")
    dwb = scatter4(lambda i: lax.dynamic_index_in_dim(dwb, i, 1, False), y, "y")
    dwa2 = dwa.astype(bf16).reshape(NY, width // NZ // NY, part)
    dwb2 = dwb.astype(bf16)
    dwa = scatter4(lambda i: lax.dynamic_index_in_dim(dwa2, i, 0, False), y, "y")
    dwb = scatter4(lambda i: lax.dynamic_index_in_dim(dwb2, i, 0, False), z, "z")
    dwab = jnp.concatenate([dwa, dwb], 1).astype(bf16).reshape(NX, -1, 2 * part)
    dwab = scatter2(lambda i: lax.dynamic_index_in_dim(dwab, i, 0, False), x)

    dact = row_product(da, wa) + row_product(db, wb)
    dact = scatter_seq([dact[j * rows : (j + 1) * rows] for j in range(N_SEQ)])
    proj = jnp.dot(swished, wo, preferred_element_type=f32)
    proj = scatter_seq([proj[j * rows : (j + 1) * rows] for j in range(N_SEQ)])
    outputs = ((xs.astype(f32) + proj) * validf).astype(bf16)
    dgain_in = jnp.sum(dact * normed, 0)
    grad_frames = (
        (own_gy.astype(f32) + norm_back(dact * gain_in, normed, inverse)) * validf
    ).astype(bf16)

    small = jnp.concatenate([dker, dgain_mid[None], dgain_in.reshape(N_SEQ, part)], 0)
    for axis in ("z", "y"):
        small = small + swap_wide(small, axis, 1) + swap_wide(small, axis, 2) + swap_wide(small, axis, 3)
    small = small + swap_wide(small, "x", 1)
    small = [small] + [swap_seq(small, d) for d in (1, 2, 3)]
    grad_gain_in = sum(a[taps_count + 1 :] for a in small).reshape(width)
    small = in_order([a[: taps_count + 1] for a in small], s)
    small = jnp.concatenate(small, 1)
    grad_kernel = small[:taps_count]
    grad_gain_mid = small[taps_count]

    share = jnp.concatenate([dwab.astype(bf16), dwo], 1)
    share = in_order(gather_seq(share), s)
    grad_w_in = jnp.concatenate(
        [a[:, :part] for a in share] + [a[:, part : 2 * part] for a in share], 1
    ).astype(f32)
    grad_w_out = jnp.concatenate([a[:, 2 * part :] for a in share], 1).astype(f32)
    return (
        outputs[None],
        grad_frames[None],
        grad_w_in,
        grad_w_out,
        grad_kernel,
        grad_gain_in,
        grad_gain_mid,
    )


def solution(mesh):
    return jax.shard_map(
        shards,
        mesh=mesh,
        in_specs=(
            P("wide", "seq", None),
            P("wide", "seq", None),
            P(),
            P("wide", None),
            P(),
            P(),
            P("wide", None),
            P("wide", "seq"),
            P("wide", "seq"),
        ),
        out_specs=(
            P("wide", "seq", None),
            P("wide", "seq", None),
            P("wide", None),
            P("wide", None),
            P(),
            P(),
            P(),
        ),
        check_vma=False,
    )
```

```python
import jax
import jax.numpy as jnp
from jax import lax
from jax.experimental import pallas as pl
from jax.experimental.pallas import tpu as pltpu
from jax.sharding import PartitionSpec as P

EPS = 1e-05
N_SEQ = 4
NZ, NY, NX = 4, 4, 2
GAP = 16
SPREAD = 768
bf16 = jnp.bfloat16
f32 = jnp.float32


def wide_index(z, y, x):
    return (z * NY + y) * NX + x


def swap_seq(value, d):
    return lax.ppermute(value, "seq", [(i, i ^ d) for i in range(N_SEQ)])


def swap_wide(value, axis, d):
    pairs = []
    for z in range(NZ):
        for y in range(NY):
            for x in range(NX):
                to = {"z": (z ^ d, y, x), "y": (z, y ^ d, x), "x": (z, y, x ^ d)}[axis]
                pairs.append((wide_index(z, y, x), wide_index(*to)))
    return lax.ppermute(value, "wide", pairs)


def after(value, *others):
    return lax.optimization_barrier((value,) + others)[0]


def swap_z_seq(value):
    pairs = []
    for s in range(N_SEQ):
        for z in range(NZ):
            for y in range(NY):
                for x in range(NX):
                    pairs.append(
                        (s * 32 + wide_index(z, y, x), z * 32 + wide_index(s, y, x))
                    )
    return lax.ppermute(value, ("seq", "wide"), pairs)


def in_order(pieces, me):
    count = len(pieces)
    d = 1
    while d < count:
        odd = (me & d) != 0
        pieces = [jnp.where(odd, pieces[j ^ d], pieces[j]) for j in range(count)]
        d *= 2
    return pieces


PLANES = [[wide_index(z, y, x) for z in range(NZ) for y in range(NY)] for x in range(NX)]


def exchange(blocks):
    return lax.all_to_all(blocks, "wide", 0, 0, axis_index_groups=PLANES, tiled=True)


def to_all(block, x):
    pair = jnp.concatenate(in_order([block, swap_wide(block, "x", 1)], x), 0)
    return pair[None]


def spread_out(pair):
    return exchange(jnp.broadcast_to(pair, (NZ * NY,) + pair.shape[1:]))


def from_all(blocks):
    return jnp.sum(exchange(blocks).astype(f32), 0)


def own_half(rows, x):
    pair = rows.reshape(NX, rows.shape[0] // NX, rows.shape[1])
    sent = lax.dynamic_index_in_dim(pair, x ^ 1, 0, False).astype(bf16)
    own = lax.dynamic_index_in_dim(pair, x, 0, False)
    return (own + swap_wide(sent, "x", 1).astype(f32)).astype(bf16)


def gather_seq(value):
    return [value] + [swap_seq(value, d) for d in (1, 2, 3)]


def layer_norm(values):
    mean = jnp.mean(values, -1, keepdims=True)
    centred = values - mean
    inverse = lax.rsqrt(jnp.mean(centred * centred, -1, keepdims=True) + EPS)
    return (centred * inverse, inverse)


def norm_back(grad, normed, inverse):
    return inverse * (
        grad
        - jnp.mean(grad, -1, keepdims=True)
        - normed * jnp.mean(grad * normed, -1, keepdims=True)
    )


def column_product(left, right):
    return lax.dot_general(left, right, (((0,), (0,)), ((), ())), preferred_element_type=f32)


def row_product(left, right):
    return lax.dot_general(left, right, (((1,), (1,)), ((), ())), preferred_element_type=f32)


def local(body, outs, *args, scalars=0, scratch=(), cost=(0, 0)):
    specs = [pl.BlockSpec(memory_space=pltpu.SMEM)] * scalars
    specs += [pl.BlockSpec(memory_space=pltpu.VMEM)] * (len(args) - scalars)
    return pl.pallas_call(
        body,
        out_shape=[jax.ShapeDtypeStruct(shape, kind) for shape, kind in outs],
        in_specs=specs,
        out_specs=[pl.BlockSpec(memory_space=pltpu.VMEM)] * len(outs),
        scratch_shapes=[pltpu.VMEM(shape, kind) for shape, kind in scratch],
        compiler_params=pltpu.CompilerParams(vmem_limit_bytes=14 * 1024 * 1024),
        cost_estimate=pl.CostEstimate(
            flops=cost[0], bytes_accessed=cost[1], transcendentals=0
        ),
        name=body.__name__,
    )(*args)


def k_norm(meta, xs, cot, gain, act, gy):
    rows, width = xs.shape
    normed, _ = layer_norm(xs[...].astype(f32))
    act[:rows] = (normed * gain[...]).astype(bf16)
    lane = lax.broadcasted_iota(jnp.int32, (16, width), 1)
    extra = jnp.zeros((16, width), f32)
    for i in range(meta.shape[0]):
        extra = jnp.where(lane == i, meta[i].astype(f32), extra)
    act[rows:] = extra.astype(bf16)
    row = lax.broadcasted_iota(jnp.int32, (rows, width), 0)
    gy[...] = jnp.where(row < meta[0], cot[...].astype(f32), 0.0).astype(bf16)


def k_place(where, a0, a1, a2, a3, act, spread, back):
    s = where[0]
    pieces = (a0, a1, a2, a3)
    rows = a0.shape[0] - 16
    metas = [a[rows : rows + 16, 0:128].astype(f32).astype(jnp.int32) for a in pieces]
    lens = [m[0:1, 0:1] for m in metas]
    bounds = [[m[0:1, i : i + 1] for i in range(1, 5)] for m in metas]
    offset = [
        n + GAP * sum((b < n).astype(jnp.int32) for b in bs) for n, bs in zip(lens, bounds)
    ]
    for j in range(N_SEQ):
        act[j * rows : (j + 1) * rows] = pieces[j][:rows]
        base = sum(((s ^ i) < (s ^ j)).astype(jnp.int32) * offset[i] for i in range(N_SEQ))
        for dim, shape in ((1, (1, rows)), (0, (rows, 1))):
            o = lax.broadcasted_iota(jnp.int32, shape, dim)
            label = sum((b <= o).astype(jnp.int32) for b in bounds[j])
            place = jnp.where(o < lens[j], base + o + GAP * label, -1)
            full = (SPREAD, rows) if dim == 1 else (rows, SPREAD)
            spots = lax.broadcasted_iota(jnp.int32, full, 1 - dim)
            hot = jnp.where(spots == place, 1.0, 0.0).astype(bf16)
            if dim == 1:
                spread[:, j * rows : (j + 1) * rows] = hot
            else:
                back[j * rows : (j + 1) * rows] = hot


def k_stack(g0, g1, g2, g3, out):
    rows = g0.shape[0]
    for j, g in enumerate((g0, g1, g2, g3)):
        out[j * rows : (j + 1) * rows] = g[...]


def shifted(x, r):
    return x if r == 0 else pltpu.roll(x, x.shape[0] - r, 0)


def k_taps(dconv, xp, dker):
    count = 31
    step = 128
    for c in range(dconv.shape[1] // 128):
        lanes = slice(c * 128, (c + 1) * 128)
        total = [jnp.zeros((8, 128), f32)] * count
        for q in range(0, dconv.shape[0], step):
            d = dconv[q : q + step, lanes]
            window = xp[q : q + step + 32, lanes]
            for r in range(8):
                moved_by = shifted(window, r)
                for k in range(count):
                    if (k + 1) % 8 == r:
                        at = k + 1 - r
                        term = d * moved_by[at : at + step]
                        total[k] = total[k] + jnp.sum(term.reshape(step // 8, 8, 128), 0)
        for k in range(count):
            dker[k : k + 1, lanes] = jnp.sum(total[k], 0, keepdims=True)


def tap_sum(xp, taps, out, store):
    count = 31
    step = 128
    for q in range(0, out.shape[0] - store[1], step):
        for c in range(xp.shape[1] // 128):
            lanes = slice(c * 128, (c + 1) * 128)
            window = xp[q : q + step + 32, lanes]
            total = jnp.zeros((step, 128), f32)
            for r in range(8):
                moved_by = shifted(window, r)
                for k in range(count):
                    if (k + 1) % 8 == r:
                        at = k + 1 - r
                        total = total + taps[k : k + 1, lanes] * moved_by[at : at + step]
            out[q + store[0] : q + store[0] + step, lanes] = total


def to_rows(first, second):
    lane = lax.broadcasted_iota(jnp.int32, (128, 128), 1)
    return jnp.transpose(jnp.where(lane == 0, first, second))[:8]


def to_columns(first, second):
    row = lax.broadcasted_iota(jnp.int32, (128, 128), 0)
    return jnp.transpose(jnp.where(row == 0, first, second))


def k_front(act, wab, spread, taps, ha, sg, xp, conv, stats, gated):
    part = ha.shape[1]
    for j in range(N_SEQ):
        at = slice(j * 128, (j + 1) * 128)
        hidden = jnp.dot(act[at], wab[...], preferred_element_type=f32)
        gate = jax.nn.sigmoid(hidden[:, part:])
        ha[at] = hidden[:, :part]
        sg[at] = gate
        gated[at] = (hidden[:, :part] * gate).astype(bf16)
    edge = jnp.zeros((16, part), f32)
    xp[0:16] = edge
    xp[16 + SPREAD :] = edge
    xp[16 : 16 + SPREAD] = jnp.dot(spread[...], gated[...], preferred_element_type=f32)
    tap_sum(xp, taps, conv, (0, 0))
    for q in range(0, SPREAD, 128):
        x = conv[q : q + 128]
        mean = jnp.mean(x, 1, keepdims=True)
        square = jnp.sum((x - mean) * (x - mean), 1, keepdims=True)
        stats[:, q : q + 128] = to_rows(mean, square)


def k_mid(stats, conv, gain, back, grad_y, normed, cols, swished, dwo, swish):
    part = conv.shape[1]
    width = part * N_SEQ
    means = [stats[i, 0:1] for i in range(N_SEQ)]
    mean = sum(means) / N_SEQ
    square = sum(stats[i, 1:2] + part * (means[i] - mean) ** 2 for i in range(N_SEQ))
    inverse = lax.rsqrt(square / width + EPS)
    for q in range(0, SPREAD, 128):
        at = slice(q, q + 128)
        col = to_columns(mean[:, at], inverse[:, at])
        cols[at] = col
        n = (conv[at] - col[:, 0:1]) * col[:, 1:2]
        normed[at] = n
        scaled = n * gain[...]
        swish[at] = (scaled * jax.nn.sigmoid(scaled)).astype(bf16)
    swished[...] = jnp.dot(back[...], swish[...], preferred_element_type=f32).astype(bf16)
    rows = part // NY
    for i in range(NZ):
        term = column_product(swished[...], grad_y[:, i * part : (i + 1) * part])
        for j in range(NY):
            dwo[i * NY + j] = term[j * rows : (j + 1) * rows].astype(bf16)


def k_grad(grad_y, wo, spread, normed, gain, grad, stats, dgain):
    part = normed.shape[1]
    ds = jnp.zeros((grad_y.shape[0], part), f32)
    for i in range(NZ):
        at = slice(i * part, (i + 1) * part)
        ds = ds + row_product(grad_y[:, at], wo[at])
    high = ds.astype(bf16)
    low = (ds - high.astype(f32)).astype(bf16)
    grad[...] = jnp.dot(spread[...], high, preferred_element_type=f32) + jnp.dot(
        spread[...], low, preferred_element_type=f32
    )
    total = jnp.zeros((1, part), f32)
    for q in range(0, SPREAD, 128):
        at = slice(q, q + 128)
        n = normed[at]
        scaled = n * gain[...]
        sig = jax.nn.sigmoid(scaled)
        d = grad[at] * sig * (1.0 + scaled * (1.0 - sig))
        total = total + jnp.sum(d * n, 0, keepdims=True)
        g = d * gain[...]
        grad[at] = g
        stats[:, at] = to_rows(
            jnp.sum(g, 1, keepdims=True), jnp.sum(g * n, 1, keepdims=True)
        )
    dgain[...] = total


def k_back(stats, grad, normed, cols, taps, ha, sg, back, act, dconv, dab, dwi, dp, dg):
    part = grad.shape[1]
    width = part * N_SEQ
    first = sum(stats[i, 0:1] for i in range(N_SEQ)) / width
    second = sum(stats[i, 1:2] for i in range(N_SEQ)) / width
    edge = jnp.zeros((16, part), f32)
    dp[0:16] = edge
    dp[16 + SPREAD :] = edge
    for q in range(0, SPREAD, 128):
        at = slice(q, q + 128)
        col = to_columns(first[:, at], second[:, at])
        d = cols[at, 1:2] * (grad[at] - col[:, 0:1] - normed[at] * col[:, 1:2])
        dconv[at] = d
        dp[q + 16 : q + 144] = d
    tap_sum(dp, taps, dg, (0, 0))
    x = dg[...]
    high = x.astype(bf16)
    low = (x - high.astype(f32)).astype(bf16)
    for j in range(N_SEQ):
        at = slice(j * 128, (j + 1) * 128)
        d = jnp.dot(back[at], high, preferred_element_type=f32) + jnp.dot(
            back[at], low, preferred_element_type=f32
        )
        gate = sg[at]
        dab[at, 0:part] = (d * gate).astype(bf16)
        dab[at, part:] = (d * ha[at] * gate * (1.0 - gate)).astype(bf16)
    for i in range(N_SEQ):
        at = slice(i * part, (i + 1) * part)
        dwi[at] = column_product(act[:, at], dab[...]).astype(bf16)


def k_dact(dab, wab, own, sent):
    rows = dab.shape[0] // N_SEQ
    for j in (1, 3, 0, 2):
        out = own if j % 2 == 0 else sent
        term = row_product(dab[j * rows : (j + 1) * rows], wab[...])
        out[j // 2] = term.astype(out.dtype)


def k_proj(swished, wo, own, sent):
    rows = swished.shape[0] // N_SEQ
    part = swished.shape[1]
    for j in range(N_SEQ):
        out = own if j % 2 == 0 else sent
        for i in range(NZ):
            at = slice(i * part, (i + 1) * part)
            term = jnp.dot(
                swished[j * rows : (j + 1) * rows], wo[at], preferred_element_type=f32
            )
            out[j // 2, :, at] = term.astype(out.dtype)


def k_forward(own, core, sent):
    sent[...] = (own[1] + core[1].astype(f32)).astype(bf16)


def k_finish(meta, xs, gy, gain, own, core, far, grads, dgain):
    rows = xs.shape[0]
    x = xs[...].astype(f32)
    valid = lax.broadcasted_iota(jnp.int32, (rows, 1), 0) < meta[0]
    dact = own[0] + core[0].astype(f32) + far[...].astype(f32)
    normed, inverse = layer_norm(x)
    dgain[...] = jnp.sum(dact * normed, 0, keepdims=True)
    dx = norm_back(dact * gain[...], normed, inverse)
    grads[...] = jnp.where(valid, gy[...].astype(f32) + dx, 0.0).astype(bf16)


def k_outputs(meta, xs, own, core, far, outputs):
    rows = xs.shape[0]
    valid = lax.broadcasted_iota(jnp.int32, (rows, 1), 0) < meta[0]
    proj = own[0] + core[0].astype(f32) + far[...].astype(f32)
    outputs[...] = jnp.where(valid, xs[...].astype(f32) + proj, 0.0).astype(bf16)


def shards(frames, cotangent, gain_in, w_in, kernel, gain_mid, w_out, group_len, starts):
    taps_count = kernel.shape[0]
    rows, width = frames.shape[1:]
    part = width // N_SEQ
    s = lax.axis_index("seq")
    wide = lax.axis_index("wide")
    z, y, x = wide // (NY * NX), (wide // NX) % NY, wide % NX
    mine = s * part

    wab = jnp.concatenate(
        [
            lax.dynamic_slice_in_dim(w_in, mine, part, 1),
            lax.dynamic_slice_in_dim(w_in, width + mine, part, 1),
        ],
        1,
    )
    pair = to_all(wab, x)
    xs = after(frames[0], wab)
    wo_pair = to_all(swap_z_seq(lax.dynamic_slice_in_dim(w_out, mine, part, 1)), x)
    wab = spread_out(pair).reshape(width, 2 * part)
    meta = jnp.concatenate([group_len[0], starts[0]])
    gain_row = gain_in[None]
    own_act, own_gy = local(
        k_norm,
        [((rows + 16, width), bf16), ((rows, width), bf16)],
        meta,
        xs,
        cotangent[0],
        gain_row,
        scalars=1,
    )
    acts = gather_seq(own_act)
    grad_ys = gather_seq(after(own_gy, acts[3]))
    act, spread, back = local(
        k_place,
        [
            ((N_SEQ * rows, width), bf16),
            ((SPREAD, N_SEQ * rows), bf16),
            ((N_SEQ * rows, SPREAD), bf16),
        ],
        s[None],
        *acts,
        scalars=1,
    )

    wo = spread_out(after(wo_pair, wab, act)).reshape(width, part)
    taps = lax.dynamic_slice_in_dim(kernel, mine, part, 1)
    gain = lax.dynamic_slice_in_dim(gain_mid, mine, part, 0)[None]
    slots = N_SEQ * rows
    ha, sg, xp, conv, stats = local(
        k_front,
        [
            ((slots, part), f32),
            ((slots, part), f32),
            ((SPREAD + 32, part), f32),
            ((SPREAD, part), f32),
            ((8, SPREAD), f32),
        ],
        act,
        wab,
        spread,
        taps,
        scratch=[((slots, part), bf16)],
    )
    stats = lax.all_gather(stats, "seq")
    grad_ys = lax.optimization_barrier((conv,) + tuple(grad_ys))[1:]
    (grad_y,) = local(k_stack, [((slots, width), bf16)], *grad_ys)
    normed, cols, swished, dwo = local(
        k_mid,
        [
            ((SPREAD, part), f32),
            ((SPREAD, 128), f32),
            ((slots, part), bf16),
            ((NZ * NY, part // NY, part), bf16),
        ],
        stats,
        conv,
        gain,
        back,
        grad_y,
        scratch=[((SPREAD, part), bf16)],
    )
    dwo = from_all(after(dwo, wo))
    grad, stats, dgain_mid = local(
        k_grad,
        [((SPREAD, part), f32), ((8, SPREAD), f32), ((1, part), f32)],
        grad_y,
        wo,
        spread,
        normed,
        gain,
    )
    stats = lax.all_gather(stats, "seq")
    dconv, dab, dwab = local(
        k_back,
        [((SPREAD, part), f32), ((slots, 2 * part), bf16), ((width, 2 * part), bf16)],
        stats,
        grad,
        normed,
        cols,
        taps[::-1],
        ha,
        sg,
        back,
        act,
        scratch=[((SPREAD + 32, part), f32), ((SPREAD, part), f32)],
    )
    dwab = after(dwab.reshape(NZ * NY, -1, 2 * part), dwo)
    dab, swished, dconv = lax.optimization_barrier((dab, swished, dconv, dwab))[:3]
    dwab = from_all(dwab)

    halves = [((2, rows, width), f32), ((2, rows, width), bf16)]
    own, sent = local(k_dact, halves, dab, wab)
    core = swap_seq(sent, 1)
    own2, sent2 = local(k_proj, halves, after(swished, sent), wo)
    core2 = swap_seq(sent2, 1)
    (sent,) = local(k_forward, [((rows, width), bf16)], own, core)
    far = swap_seq(sent, 2)
    (sent2,) = local(k_forward, [((rows, width), bf16)], own2, core2)
    far2 = swap_seq(sent2, 2)
    (dker,) = local(k_taps, [((taps_count, part), f32)], after(dconv, sent2), xp)
    own = after(own, dker)
    grad_frames, dgain_in = local(
        k_finish,
        [((rows, width), bf16), ((1, width), f32)],
        meta,
        xs,
        own_gy,
        gain_row,
        own,
        core,
        far,
        scalars=1,
    )
    (outputs,) = local(
        k_outputs, [((rows, width), bf16)], meta, xs, own2, core2, far2, scalars=1
    )
    dwo = swap_z_seq(own_half(dwo, x))
    small = jnp.concatenate([dker, dgain_mid, dgain_in.reshape(N_SEQ, part)], 0)
    small = small + swap_wide(small, "x", 1)
    dwab = own_half(dwab, x)
    for axis in ("z", "y"):
        if axis == "y":
            small = after(small, dwab)
        small = (small + swap_wide(small, axis, 1)) + (
            swap_wide(small, axis, 2) + swap_wide(small, axis, 3)
        )
    small = [small] + [swap_seq(small, d) for d in (1, 2, 3)]
    grad_gain_in = sum(a[taps_count + 1 :] for a in small).reshape(width)
    small = in_order([a[: taps_count + 1] for a in small], s)
    small = jnp.concatenate(small, 1)
    grad_kernel = small[:taps_count]
    grad_gain_mid = small[taps_count]

    share = jnp.concatenate([dwab, dwo], 1)
    share = in_order(gather_seq(share), s)
    grad_w_in = jnp.concatenate(
        [a[:, :part] for a in share] + [a[:, part : 2 * part] for a in share], 1
    ).astype(f32)
    grad_w_out = jnp.concatenate([a[:, 2 * part :] for a in share], 1).astype(f32)
    return (
        outputs[None],
        grad_frames[None],
        grad_w_in,
        grad_w_out,
        grad_kernel,
        grad_gain_in,
        grad_gain_mid,
    )


def solution(mesh):
    return jax.shard_map(
        shards,
        mesh=mesh,
        in_specs=(
            P("wide", "seq", None),
            P("wide", "seq", None),
            P(),
            P("wide", None),
            P(),
            P(),
            P("wide", None),
            P("wide", "seq"),
            P("wide", "seq"),
        ),
        out_specs=(
            P("wide", "seq", None),
            P("wide", "seq", None),
            P("wide", None),
            P("wide", None),
            P(),
            P(),
            P(),
        ),
        check_vma=False,
    )
```

```python
import jax
import jax.numpy as jnp
from jax import lax
from jax.experimental import pallas as pl
from jax.experimental.pallas import tpu as pltpu
from jax.sharding import PartitionSpec as P

EPS = 1e-05
N_SEQ = 4
NZ, NY, NX = 4, 4, 2
GAP = 16
SPREAD = 768
bf16 = jnp.bfloat16
f32 = jnp.float32


def wide_index(z, y, x):
    return (z * NY + y) * NX + x


def swap_seq(value, d):
    return lax.ppermute(value, "seq", [(i, i ^ d) for i in range(N_SEQ)])


def swap_wide(value, axis, d):
    pairs = []
    for z in range(NZ):
        for y in range(NY):
            for x in range(NX):
                to = {"z": (z ^ d, y, x), "y": (z, y ^ d, x), "x": (z, y, x ^ d)}[axis]
                pairs.append((wide_index(z, y, x), wide_index(*to)))
    return lax.ppermute(value, "wide", pairs)


def after(value, *others):
    return lax.optimization_barrier((value,) + others)[0]


def swap_z_seq(value):
    pairs = []
    for s in range(N_SEQ):
        for z in range(NZ):
            for y in range(NY):
                for x in range(NX):
                    pairs.append(
                        (s * 32 + wide_index(z, y, x), z * 32 + wide_index(s, y, x))
                    )
    return lax.ppermute(value, ("seq", "wide"), pairs)


def in_order(pieces, me):
    count = len(pieces)
    d = 1
    while d < count:
        odd = (me & d) != 0
        pieces = [jnp.where(odd, pieces[j ^ d], pieces[j]) for j in range(count)]
        d *= 2
    return pieces


PLANES = [[wide_index(z, y, x) for z in range(NZ) for y in range(NY)] for x in range(NX)]


def exchange(blocks):
    return lax.all_to_all(blocks, "wide", 0, 0, axis_index_groups=PLANES, tiled=True)


def to_all(block, x):
    pair = jnp.concatenate(in_order([block, swap_wide(block, "x", 1)], x), 0)
    return pair[None]


def spread_out(pair):
    return exchange(jnp.broadcast_to(pair, (NZ * NY,) + pair.shape[1:]))


def from_all(blocks):
    return jnp.sum(exchange(blocks).astype(f32), 0)


def own_half(rows, x):
    pair = rows.reshape(NX, rows.shape[0] // NX, rows.shape[1])
    sent = lax.dynamic_index_in_dim(pair, x ^ 1, 0, False).astype(bf16)
    own = lax.dynamic_index_in_dim(pair, x, 0, False)
    return (own + swap_wide(sent, "x", 1).astype(f32)).astype(bf16)


def gather_seq(value):
    far = swap_seq(value, 2)
    return [value, swap_seq(value, 1), far, swap_seq(far, 1)]


def layer_norm(values):
    mean = jnp.mean(values, -1, keepdims=True)
    centred = values - mean
    inverse = lax.rsqrt(jnp.mean(centred * centred, -1, keepdims=True) + EPS)
    return (centred * inverse, inverse)


def norm_back(grad, normed, inverse):
    return inverse * (
        grad
        - jnp.mean(grad, -1, keepdims=True)
        - normed * jnp.mean(grad * normed, -1, keepdims=True)
    )


def column_product(left, right):
    return lax.dot_general(left, right, (((0,), (0,)), ((), ())), preferred_element_type=f32)


def row_product(left, right):
    return lax.dot_general(left, right, (((1,), (1,)), ((), ())), preferred_element_type=f32)


def local(body, outs, *args, scalars=0, scratch=(), sems=0, cost=(0, 0)):
    place = pl.BlockSpec(memory_space=pl.ANY if sems else pltpu.VMEM)
    specs = [pl.BlockSpec(memory_space=pltpu.SMEM)] * scalars
    specs += [place] * (len(args) - scalars)
    return pl.pallas_call(
        body,
        out_shape=[jax.ShapeDtypeStruct(shape, kind) for shape, kind in outs],
        in_specs=specs,
        out_specs=[place] * len(outs),
        scratch_shapes=[pltpu.VMEM(shape, kind) for shape, kind in scratch]
        + [pltpu.SemaphoreType.DMA((sems,))] * (sems > 0),
        compiler_params=pltpu.CompilerParams(vmem_limit_bytes=14 * 1024 * 1024),
        cost_estimate=pl.CostEstimate(
            flops=cost[0], bytes_accessed=cost[1], transcendentals=0
        ),
        name=body.__name__,
    )(*args)


def k_norm(meta, xs, cot, gain, out):
    rows, width = xs.shape
    normed, _ = layer_norm(xs[...].astype(f32))
    out[:rows] = (normed * gain[...]).astype(bf16)
    lane = lax.broadcasted_iota(jnp.int32, (16, width), 1)
    extra = jnp.zeros((16, width), f32)
    for i in range(meta.shape[0]):
        extra = jnp.where(lane == i, meta[i].astype(f32), extra)
    out[rows : rows + 16] = extra.astype(bf16)
    row = lax.broadcasted_iota(jnp.int32, (rows, width), 0)
    out[rows + 16 :] = jnp.where(row < meta[0], cot[...].astype(f32), 0.0).astype(bf16)


def manual(body, outs, *args, scalars=0, fast=0, scratch=(), sems=0):
    vmem = pl.BlockSpec(memory_space=pltpu.VMEM)
    large = pl.BlockSpec(memory_space=pl.ANY)
    specs = [pl.BlockSpec(memory_space=pltpu.SMEM)] * scalars + [vmem] * fast
    specs += [large] * (len(args) - scalars - fast)
    return pl.pallas_call(
        body,
        out_shape=[jax.ShapeDtypeStruct(o[0], o[1]) for o in outs],
        in_specs=specs,
        out_specs=[vmem if len(o) > 2 else large for o in outs],
        scratch_shapes=[pltpu.VMEM(shape, kind) for shape, kind in scratch]
        + [pltpu.SemaphoreType.DMA((sems,))],
        compiler_params=pltpu.CompilerParams(vmem_limit_bytes=60 * 1024 * 1024),
        cost_estimate=pl.CostEstimate(flops=0, bytes_accessed=0, transcendentals=0),
        name=body.__name__,
    )(*args)


def begin(sems, first, pairs):
    copies = [
        pltpu.make_async_copy(a, b, sems.at[first + i]) for i, (a, b) in enumerate(pairs)
    ]
    for c in copies:
        c.start()
    return copies


def finish(copies):
    for c in copies:
        c.wait()


def to_spread(places, out):
    for j in range(out.shape[1] // 128):
        at = slice(j * 128, (j + 1) * 128)
        spots = lax.broadcasted_iota(jnp.int32, (out.shape[0], 128), 0).astype(f32)
        out[:, at] = jnp.where(spots == places[0:1, at], 1.0, 0.0).astype(bf16)


def to_back(places, out):
    for j in range(out.shape[0] // 128):
        at = slice(j * 128, (j + 1) * 128)
        column = jnp.transpose(jnp.broadcast_to(places[0:1, at], (128, 128)))[:, 0:1]
        spots = lax.broadcasted_iota(jnp.int32, (128, out.shape[1]), 1).astype(f32)
        out[at] = jnp.where(spots == column, 1.0, 0.0).astype(bf16)


def shifted(x, r):
    return x if r == 0 else pltpu.roll(x, x.shape[0] - r, 0)


def k_taps(dconv, xp, dker):
    count = 31
    step = 128
    for c in range(dconv.shape[1] // 128):
        lanes = slice(c * 128, (c + 1) * 128)
        total = [jnp.zeros((8, 128), f32)] * count
        for q in range(0, dconv.shape[0], step):
            d = dconv[q : q + step, lanes]
            window = xp[q : q + step + 32, lanes]
            for r in range(8):
                moved_by = shifted(window, r)
                for k in range(count):
                    if (k + 1) % 8 == r:
                        at = k + 1 - r
                        term = d * moved_by[at : at + step]
                        total[k] = total[k] + jnp.sum(term.reshape(step // 8, 8, 128), 0)
        for k in range(count):
            dker[k : k + 1, lanes] = jnp.sum(total[k], 0, keepdims=True)


def tap_sum(xp, taps, out, store):
    count = 31
    step = 128
    for q in range(0, out.shape[0] - store[1], step):
        for c in range(xp.shape[1] // 128):
            lanes = slice(c * 128, (c + 1) * 128)
            window = xp[q : q + step + 32, lanes]
            total = jnp.zeros((step, 128), f32)
            for r in range(8):
                moved_by = shifted(window, r)
                for k in range(count):
                    if (k + 1) % 8 == r:
                        at = k + 1 - r
                        total = total + taps[k : k + 1, lanes] * moved_by[at : at + step]
            out[q + store[0] : q + store[0] + step, lanes] = total


def to_rows(first, second):
    lane = lax.broadcasted_iota(jnp.int32, (128, 128), 1)
    return jnp.transpose(jnp.where(lane == 0, first, second))[:8]


def to_columns(first, second):
    row = lax.broadcasted_iota(jnp.int32, (128, 128), 0)
    return jnp.transpose(jnp.where(row == 0, first, second))


def k_front(
    where, taps, a0, a1, a2, a3, wab, ha, sg, xp, conv, stats, places,
    acts, heads, w, has, sgs, xps, convs, gated, spread, sems,
):
    s = where[0]
    rows = acts.shape[0] // N_SEQ
    part = has.shape[1]
    pieces = (a0, a1, a2, a3)
    loads = begin(
        sems, 9, [(a.at[pl.ds(rows, 16), pl.ds(0, 128)], heads.at[j]) for j, a in enumerate(pieces)]
    )
    weights = begin(sems, 4, [(wab, w)]) + begin(
        sems,
        0,
        [(a.at[pl.ds(0, rows)], acts.at[pl.ds(j * rows, rows)]) for j, a in enumerate(pieces)],
    )
    edge = jnp.zeros((16, part), f32)
    xps[0:16] = edge
    xps[16 + SPREAD :] = edge
    finish(loads)
    metas = [heads[j].astype(f32).astype(jnp.int32) for j in range(N_SEQ)]
    lens = [m[0:1, 0:1] for m in metas]
    bounds = [[m[0:1, i : i + 1] for i in range(1, 5)] for m in metas]
    offset = [
        n + GAP * sum((b < n).astype(jnp.int32) for b in bs) for n, bs in zip(lens, bounds)
    ]
    for j in range(N_SEQ):
        base = sum(((s ^ i) < (s ^ j)).astype(jnp.int32) * offset[i] for i in range(N_SEQ))
        o = lax.broadcasted_iota(jnp.int32, (8, rows), 1)
        label = sum((b <= o).astype(jnp.int32) for b in bounds[j])
        place = jnp.where(o < lens[j], base + o + GAP * label, -1)
        places[:, j * rows : (j + 1) * rows] = place.astype(f32)
    to_spread(places, spread)
    finish(weights)
    hidden = jnp.dot(acts[...], w[...], preferred_element_type=f32)
    gate = jax.nn.sigmoid(hidden[:, part:])
    has[...] = hidden[:, :part]
    sgs[...] = gate
    gated[...] = (hidden[:, :part] * gate).astype(bf16)
    stores = begin(sems, 5, [(has, ha), (sgs, sg)])
    xps[16 : 16 + SPREAD] = jnp.dot(spread[...], gated[...], preferred_element_type=f32)
    stores += begin(sems, 7, [(xps, xp)])
    tap_sum(xps, taps, convs, (0, 0))
    stores += begin(sems, 8, [(convs, conv)])
    for q in range(0, SPREAD, 128):
        x = convs[q : q + 128]
        mean = jnp.mean(x, 1, keepdims=True)
        square = jnp.sum((x - mean) * (x - mean), 1, keepdims=True)
        stats[:, q : q + 128] = to_rows(mean, square)
    finish(stores)


def load_grad_y(sems, pieces, out):
    rows = out.shape[0] // N_SEQ
    return begin(
        sems,
        0,
        [
            (p.at[pl.ds(rows + 16, rows)], out.at[pl.ds(j * rows, rows)])
            for j, p in enumerate(pieces)
        ],
    )


def k_mid(
    gain, stats, places, a0, a1, a2, a3, conv, swished, dwo, lines,
    gy, convs, swish, back, sw, dws, sems,
):
    part = convs.shape[1]
    width = part * N_SEQ
    first = begin(sems, 4, [(conv, convs)])
    loads = load_grad_y(sems, (a0, a1, a2, a3), gy)
    means = [stats[i, 0:1] for i in range(N_SEQ)]
    mean = sum(means) / N_SEQ
    square = sum(stats[i, 1:2] + part * (means[i] - mean) ** 2 for i in range(N_SEQ))
    inverse = lax.rsqrt(square / width + EPS)
    row = lax.broadcasted_iota(jnp.int32, (8, SPREAD), 0)
    lines[...] = jnp.where(row == 0, mean, inverse)
    to_back(places, back)
    finish(first)
    for q in range(0, SPREAD, 128):
        at = slice(q, q + 128)
        col = to_columns(mean[:, at], inverse[:, at])
        scaled = (convs[at] - col[:, 0:1]) * col[:, 1:2] * gain[...]
        swish[at] = (scaled * jax.nn.sigmoid(scaled)).astype(bf16)
    sw[...] = jnp.dot(back[...], swish[...], preferred_element_type=f32).astype(bf16)
    stores = begin(sems, 5, [(sw, swished)])
    finish(loads)
    rows = part // NY
    for i in range(NZ):
        term = column_product(sw[...], gy[:, i * part : (i + 1) * part])
        for j in range(NY):
            dws[i * NY + j] = term[j * rows : (j + 1) * rows].astype(bf16)
    stores += begin(sems, 6, [(dws, dwo)])
    finish(stores)


def k_grad(
    gain, lines, places, a0, a1, a2, a3, wo, conv, grad, stats, dgain,
    gy, w, convs, spread, grads, sems,
):
    part = convs.shape[1]
    loads = load_grad_y(sems, (a0, a1, a2, a3), gy)
    loads += begin(sems, 4, [(wo, w)])
    second = begin(sems, 5, [(conv, convs)])
    to_spread(places, spread)
    finish(loads)
    ds = jnp.zeros((gy.shape[0], part), f32)
    for i in range(NZ):
        at = slice(i * part, (i + 1) * part)
        ds = ds + row_product(gy[:, at], w[at])
    high = ds.astype(bf16)
    low = (ds - high.astype(f32)).astype(bf16)
    grads[...] = jnp.dot(spread[...], high, preferred_element_type=f32) + jnp.dot(
        spread[...], low, preferred_element_type=f32
    )
    finish(second)
    total = jnp.zeros((1, part), f32)
    for q in range(0, SPREAD, 128):
        at = slice(q, q + 128)
        col = to_columns(lines[0:1, at], lines[1:2, at])
        n = (convs[at] - col[:, 0:1]) * col[:, 1:2]
        scaled = n * gain[...]
        sig = jax.nn.sigmoid(scaled)
        d = grads[at] * sig * (1.0 + scaled * (1.0 - sig))
        total = total + jnp.sum(d * n, 0, keepdims=True)
        g = d * gain[...]
        grads[at] = g
        stats[:, at] = to_rows(
            jnp.sum(g, 1, keepdims=True), jnp.sum(g * n, 1, keepdims=True)
        )
    stores = begin(sems, 6, [(grads, grad)])
    dgain[...] = total
    finish(stores)


def k_back(
    stats, lines, places, taps, a0, a1, a2, a3, conv, grad, ha, sg, dconv, dab, dwi,
    convs, grads, acts, has, sgs, dp, dg, back, ds, dws, sems,
):
    part = convs.shape[1]
    width = part * N_SEQ
    rows = acts.shape[0] // N_SEQ
    loads = begin(sems, 0, [(conv, convs), (grad, grads)])
    gates = begin(sems, 2, [(ha, has), (sg, sgs)])
    later = begin(
        sems,
        4,
        [
            (a.at[pl.ds(0, rows)], acts.at[pl.ds(j * rows, rows)])
            for j, a in enumerate((a0, a1, a2, a3))
        ],
    )
    to_back(places, back)
    first = sum(stats[i, 0:1] for i in range(N_SEQ)) / width
    second = sum(stats[i, 1:2] for i in range(N_SEQ)) / width
    edge = jnp.zeros((16, part), f32)
    dp[0:16] = edge
    dp[16 + SPREAD :] = edge
    finish(loads)
    for q in range(0, SPREAD, 128):
        at = slice(q, q + 128)
        line = to_columns(lines[0:1, at], lines[1:2, at])
        col = to_columns(first[:, at], second[:, at])
        n = (convs[at] - line[:, 0:1]) * line[:, 1:2]
        dp[q + 16 : q + 144] = line[:, 1:2] * (grads[at] - col[:, 0:1] - n * col[:, 1:2])
    stores = begin(sems, 8, [(dp.at[pl.ds(16, SPREAD)], dconv)])
    tap_sum(dp, taps, dg, (0, 0))
    x = dg[...]
    high = x.astype(bf16)
    low = (x - high.astype(f32)).astype(bf16)
    finish(gates)
    d = jnp.dot(back[...], high, preferred_element_type=f32) + jnp.dot(
        back[...], low, preferred_element_type=f32
    )
    gate = sgs[...]
    ds[:, 0:part] = (d * gate).astype(bf16)
    ds[:, part:] = (d * has[...] * gate * (1.0 - gate)).astype(bf16)
    stores += begin(sems, 9, [(ds, dab)])
    finish(later)
    for i in range(N_SEQ):
        at = slice(i * part, (i + 1) * part)
        dws[at] = column_product(acts[:, at], ds[...]).astype(bf16)
        block = pl.ds(i * part, part)
        stores += begin(sems, 10 + i, [(dws.at[block], dwi.at[block])])
    finish(stores)


def k_dact(dab, wab, own, sent):
    rows = dab.shape[0] // N_SEQ
    term = row_product(dab[...], wab[...])
    for j in range(N_SEQ):
        out = own if j % 2 == 0 else sent
        out[j // 2] = term[j * rows : (j + 1) * rows].astype(out.dtype)


def k_proj(swished, wo, own, sent):
    rows = swished.shape[0] // N_SEQ
    part = swished.shape[1]
    for i in range(NZ):
        at = slice(i * part, (i + 1) * part)
        term = jnp.dot(swished[...], wo[at], preferred_element_type=f32)
        for j in range(N_SEQ):
            out = own if j % 2 == 0 else sent
            out[j // 2, :, at] = term[j * rows : (j + 1) * rows].astype(out.dtype)


def k_forward(own, core, sent):
    sent[...] = (own[1] + core[1].astype(f32)).astype(bf16)


def k_finish(meta, xs, gy, gain, own, core, far, grads, dgain):
    rows = xs.shape[0]
    x = xs[...].astype(f32)
    valid = lax.broadcasted_iota(jnp.int32, (rows, 1), 0) < meta[0]
    dact = own[0] + core[0].astype(f32) + far[...].astype(f32)
    normed, inverse = layer_norm(x)
    dgain[...] = jnp.sum(dact * normed, 0, keepdims=True)
    dx = norm_back(dact * gain[...], normed, inverse)
    grads[...] = jnp.where(valid, gy[rows + 16 :].astype(f32) + dx, 0.0).astype(bf16)


def k_outputs(meta, xs, own, core, far, outputs):
    rows = xs.shape[0]
    valid = lax.broadcasted_iota(jnp.int32, (rows, 1), 0) < meta[0]
    proj = own[0] + core[0].astype(f32) + far[...].astype(f32)
    outputs[...] = jnp.where(valid, xs[...].astype(f32) + proj, 0.0).astype(bf16)


def shards(frames, cotangent, gain_in, w_in, kernel, gain_mid, w_out, group_len, starts):
    taps_count = kernel.shape[0]
    rows, width = frames.shape[1:]
    part = width // N_SEQ
    s = lax.axis_index("seq")
    wide = lax.axis_index("wide")
    z, y, x = wide // (NY * NX), (wide // NX) % NY, wide % NX
    mine = s * part

    wab = jnp.concatenate(
        [
            lax.dynamic_slice_in_dim(w_in, mine, part, 1),
            lax.dynamic_slice_in_dim(w_in, width + mine, part, 1),
        ],
        1,
    )
    pair = to_all(wab, x)
    wo = swap_z_seq(lax.dynamic_slice_in_dim(w_out, mine, part, 1))
    xs = frames[0]

    meta = jnp.concatenate([group_len[0], starts[0]])
    gain_row = gain_in[None]
    (own_rows,) = local(
        k_norm,
        [((2 * rows + 16, width), bf16)],
        meta,
        xs,
        cotangent[0],
        gain_row,
        scalars=1,
    )
    wab = spread_out(after(pair, own_rows)).reshape(width, 2 * part)
    pieces = gather_seq(own_rows)
    taps = lax.dynamic_slice_in_dim(kernel, mine, part, 1)
    gain = lax.dynamic_slice_in_dim(gain_mid, mine, part, 0)[None]
    slots = N_SEQ * rows
    wide_f32, slot_f32 = ((SPREAD, part), f32), ((slots, part), f32)
    rows_f32, padded_f32 = ((8, SPREAD), f32, True), ((SPREAD + 32, part), f32)
    hot, hot_back = ((SPREAD, slots), bf16), ((slots, SPREAD), bf16)
    all_rows, slot_bf16 = ((slots, width), bf16), ((slots, part), bf16)
    ha, sg, xp, conv, stats, places = manual(
        k_front,
        [slot_f32, slot_f32, padded_f32, wide_f32, rows_f32, ((8, slots), f32, True)],
        s[None],
        taps,
        *pieces,
        wab,
        scalars=1,
        fast=1,
        scratch=[
            all_rows,
            ((N_SEQ, 16, 128), bf16),
            ((width, 2 * part), bf16),
            slot_f32,
            slot_f32,
            padded_f32,
            wide_f32,
            slot_bf16,
            hot,
        ],
        sems=13,
    )
    wo_pair = to_all(after(wo, pieces[2]), x)
    wo = spread_out(after(wo_pair, wab, stats)).reshape(width, part)
    stats = lax.all_gather(stats, "seq")
    blocks = ((NZ * NY, part // NY, part), bf16)
    swished, dwo, lines = manual(
        k_mid,
        [slot_bf16, blocks, rows_f32],
        gain,
        stats,
        places,
        *pieces,
        conv,
        fast=3,
        scratch=[all_rows, wide_f32, ((SPREAD, part), bf16), hot_back, slot_bf16, blocks],
        sems=7,
    )
    dwo = from_all(after(dwo, wo))
    grad, stats, dgain_mid = manual(
        k_grad,
        [wide_f32, rows_f32, ((1, part), f32, True)],
        gain,
        lines,
        places,
        *pieces,
        wo,
        conv,
        fast=3,
        scratch=[all_rows, ((width, part), bf16), wide_f32, hot, wide_f32],
        sems=7,
    )
    stats = lax.all_gather(stats, "seq")
    both, weights = ((slots, 2 * part), bf16), ((width, 2 * part), bf16)
    dconv, dab, dwab = manual(
        k_back,
        [wide_f32, both, weights],
        stats,
        lines,
        places,
        taps[::-1],
        *pieces,
        conv,
        grad,
        ha,
        sg,
        fast=4,
        scratch=[
            wide_f32,
            wide_f32,
            all_rows,
            slot_f32,
            slot_f32,
            padded_f32,
            wide_f32,
            hot_back,
            both,
            weights,
        ],
        sems=14,
    )
    dwab = after(dwab.reshape(NZ * NY, -1, 2 * part), dwo)
    dab, swished, dconv = lax.optimization_barrier((dab, swished, dconv, dwab))[:3]
    dwab = from_all(dwab)

    halves = [((2, rows, width), f32), ((2, rows, width), bf16)]
    own, sent = local(k_dact, halves, dab, wab)
    core = swap_seq(sent, 1)
    dwo = own_half(dwo, x)
    own2, sent2 = local(k_proj, halves, after(swished, sent), wo)
    core2 = swap_seq(sent2, 1)
    (sent,) = local(k_forward, [((rows, width), bf16)], own, core)
    far = swap_seq(sent, 2)
    (sent2,) = local(k_forward, [((rows, width), bf16)], own2, core2)
    far2 = swap_seq(sent2, 2)
    (dker,) = local(k_taps, [((taps_count, part), f32)], after(dconv, sent2), xp)
    own = after(own, dker)
    grad_frames, dgain_in = local(
        k_finish,
        [((rows, width), bf16), ((1, width), f32)],
        meta,
        xs,
        own_rows,
        gain_row,
        own,
        core,
        far,
        scalars=1,
    )
    (outputs,) = local(
        k_outputs, [((rows, width), bf16)], meta, xs, own2, core2, far2, scalars=1
    )
    small = jnp.concatenate([dker, dgain_mid, dgain_in.reshape(N_SEQ, part)], 0)
    small = small + swap_wide(small, "x", 1)
    dwo = swap_z_seq(after(dwo, dwab))
    dwab = own_half(dwab, x)
    for axis in ("z", "y"):
        if axis == "y":
            small = after(small, dwab)
        small = (small + swap_wide(small, axis, 1)) + (
            swap_wide(small, axis, 2) + swap_wide(small, axis, 3)
        )
    small = [small] + [swap_seq(small, d) for d in (1, 2, 3)]
    total = (small[0] + small[1]) + (small[2] + small[3])
    grad_gain_in = total[taps_count + 1 :].reshape(width)
    small = in_order([a[: taps_count + 1] for a in small], s)
    small = jnp.concatenate(small, 1)
    grad_kernel = small[:taps_count]
    grad_gain_mid = small[taps_count]

    share = jnp.concatenate([dwab, dwo], 1)
    share = in_order([share] + [swap_seq(share, d) for d in (1, 2, 3)], s)
    grad_w_in = jnp.concatenate(
        [a[:, :part] for a in share] + [a[:, part : 2 * part] for a in share], 1
    ).astype(f32)
    grad_w_out = jnp.concatenate([a[:, 2 * part :] for a in share], 1).astype(f32)
    return (
        outputs[None],
        grad_frames[None],
        grad_w_in,
        grad_w_out,
        grad_kernel,
        grad_gain_in,
        grad_gain_mid,
    )


def solution(mesh):
    return jax.shard_map(
        shards,
        mesh=mesh,
        in_specs=(
            P("wide", "seq", None),
            P("wide", "seq", None),
            P(),
            P("wide", None),
            P(),
            P(),
            P("wide", None),
            P("wide", "seq"),
            P("wide", "seq"),
        ),
        out_specs=(
            P("wide", "seq", None),
            P("wide", "seq", None),
            P("wide", None),
            P("wide", None),
            P(),
            P(),
            P(),
        ),
        check_vma=False,
    )
```

```python
import jax
import jax.numpy as jnp
from jax import lax
from jax.experimental import pallas as pl
from jax.experimental.pallas import tpu as pltpu
from jax.sharding import PartitionSpec as P

EPS = 1e-05
N_SEQ = 4
NZ, NY, NX = 4, 4, 2
GAP = 16
SPREAD = 768
bf16 = jnp.bfloat16
f32 = jnp.float32


def wide_index(z, y, x):
    return (z * NY + y) * NX + x


def swap_seq(value, d):
    return lax.ppermute(value, "seq", [(i, i ^ d) for i in range(N_SEQ)])


def swap_wide(value, axis, d):
    pairs = []
    for z in range(NZ):
        for y in range(NY):
            for x in range(NX):
                to = {"z": (z ^ d, y, x), "y": (z, y ^ d, x), "x": (z, y, x ^ d)}[axis]
                pairs.append((wide_index(z, y, x), wide_index(*to)))
    return lax.ppermute(value, "wide", pairs)


def after(value, *others):
    return lax.optimization_barrier((value,) + others)[0]


def swap_z_seq(value):
    pairs = []
    for s in range(N_SEQ):
        for z in range(NZ):
            for y in range(NY):
                for x in range(NX):
                    pairs.append(
                        (s * 32 + wide_index(z, y, x), z * 32 + wide_index(s, y, x))
                    )
    return lax.ppermute(value, ("seq", "wide"), pairs)


def in_order(pieces, me):
    count = len(pieces)
    d = 1
    while d < count:
        odd = (me & d) != 0
        pieces = [jnp.where(odd, pieces[j ^ d], pieces[j]) for j in range(count)]
        d *= 2
    return pieces


PLANES = [[wide_index(z, y, x) for z in range(NZ) for y in range(NY)] for x in range(NX)]


def exchange(blocks):
    return lax.all_to_all(blocks, "wide", 0, 0, axis_index_groups=PLANES, tiled=True)


def to_all(block, x):
    pair = jnp.concatenate(in_order([block, swap_wide(block, "x", 1)], x), 0)
    return pair[None]


def copies(pair):
    return jnp.broadcast_to(pair, (NZ * NY,) + pair.shape[1:])


def from_all(blocks):
    return jnp.sum(exchange(blocks).astype(f32), 0)


def own_half(rows, x):
    pair = rows.reshape(NX, rows.shape[0] // NX, rows.shape[1])
    sent = lax.dynamic_index_in_dim(pair, x ^ 1, 0, False).astype(bf16)
    own = lax.dynamic_index_in_dim(pair, x, 0, False)
    return (own + swap_wide(sent, "x", 1).astype(f32)).astype(bf16)


def gather_seq(value):
    far = swap_seq(value, 2)
    return [value, swap_seq(value, 1), far, swap_seq(far, 1)]


def layer_norm(values):
    mean = jnp.mean(values, -1, keepdims=True)
    centred = values - mean
    inverse = lax.rsqrt(jnp.mean(centred * centred, -1, keepdims=True) + EPS)
    return (centred * inverse, inverse)


def norm_back(grad, normed, inverse):
    return inverse * (
        grad
        - jnp.mean(grad, -1, keepdims=True)
        - normed * jnp.mean(grad * normed, -1, keepdims=True)
    )


def column_product(left, right):
    return lax.dot_general(left, right, (((0,), (0,)), ((), ())), preferred_element_type=f32)


def row_product(left, right):
    return lax.dot_general(left, right, (((1,), (1,)), ((), ())), preferred_element_type=f32)


def local(body, outs, *args, scalars=0, scratch=(), sems=0, cost=(0, 0)):
    place = pl.BlockSpec(memory_space=pl.ANY if sems else pltpu.VMEM)
    specs = [pl.BlockSpec(memory_space=pltpu.SMEM)] * scalars
    specs += [place] * (len(args) - scalars)
    return pl.pallas_call(
        body,
        out_shape=[jax.ShapeDtypeStruct(shape, kind) for shape, kind in outs],
        in_specs=specs,
        out_specs=[place] * len(outs),
        scratch_shapes=[pltpu.VMEM(shape, kind) for shape, kind in scratch]
        + [pltpu.SemaphoreType.DMA((sems,))] * (sems > 0),
        compiler_params=pltpu.CompilerParams(vmem_limit_bytes=14 * 1024 * 1024),
        cost_estimate=pl.CostEstimate(
            flops=cost[0], bytes_accessed=cost[1], transcendentals=0
        ),
        name=body.__name__,
    )(*args)


def k_norm(meta, xs, cot, gain, out):
    rows, width = xs.shape
    normed, _ = layer_norm(xs[...].astype(f32))
    out[:rows] = (normed * gain[...]).astype(bf16)
    lane = lax.broadcasted_iota(jnp.int32, (16, width), 1)
    extra = jnp.zeros((16, width), f32)
    for i in range(meta.shape[0]):
        extra = jnp.where(lane == i, meta[i].astype(f32), extra)
    out[rows : rows + 16] = extra.astype(bf16)
    row = lax.broadcasted_iota(jnp.int32, (rows, width), 0)
    out[rows + 16 :] = jnp.where(row < meta[0], cot[...].astype(f32), 0.0).astype(bf16)


def manual(body, outs, *args, scalars=0, fast=0, scratch=(), sems=0):
    vmem = pl.BlockSpec(memory_space=pltpu.VMEM)
    large = pl.BlockSpec(memory_space=pl.ANY)
    specs = [pl.BlockSpec(memory_space=pltpu.SMEM)] * scalars + [vmem] * fast
    specs += [large] * (len(args) - scalars - fast)
    return pl.pallas_call(
        body,
        out_shape=[jax.ShapeDtypeStruct(o[0], o[1]) for o in outs],
        in_specs=specs,
        out_specs=[vmem if len(o) > 2 else large for o in outs],
        scratch_shapes=[pltpu.VMEM(shape, kind) for shape, kind in scratch]
        + [pltpu.SemaphoreType.DMA((sems,))],
        compiler_params=pltpu.CompilerParams(vmem_limit_bytes=60 * 1024 * 1024),
        cost_estimate=pl.CostEstimate(flops=0, bytes_accessed=0, transcendentals=0),
        name=body.__name__,
    )(*args)


def begin(sems, first, pairs):
    copies = [
        pltpu.make_async_copy(a, b, sems.at[first + i]) for i, (a, b) in enumerate(pairs)
    ]
    for c in copies:
        c.start()
    return copies


def finish(copies):
    for c in copies:
        c.wait()


def to_spread(places, out):
    for j in range(out.shape[1] // 128):
        at = slice(j * 128, (j + 1) * 128)
        spots = lax.broadcasted_iota(jnp.int32, (out.shape[0], 128), 0).astype(f32)
        out[:, at] = jnp.where(spots == places[0:1, at], 1.0, 0.0).astype(bf16)


def to_back(places, out):
    for j in range(out.shape[0] // 128):
        at = slice(j * 128, (j + 1) * 128)
        column = jnp.transpose(jnp.broadcast_to(places[0:1, at], (128, 128)))[:, 0:1]
        spots = lax.broadcasted_iota(jnp.int32, (128, out.shape[1]), 1).astype(f32)
        out[at] = jnp.where(spots == column, 1.0, 0.0).astype(bf16)


def shifted(x, r):
    return x if r == 0 else pltpu.roll(x, x.shape[0] - r, 0)


def k_taps(dconv, xp, dker):
    count = 31
    step = 128
    for c in range(dconv.shape[1] // 128):
        lanes = slice(c * 128, (c + 1) * 128)
        total = [jnp.zeros((8, 128), f32)] * count
        for q in range(0, dconv.shape[0], step):
            d = dconv[q : q + step, lanes]
            window = xp[q : q + step + 32, lanes]
            for r in range(8):
                moved_by = shifted(window, r)
                for k in range(count):
                    if (k + 1) % 8 == r:
                        at = k + 1 - r
                        term = d * moved_by[at : at + step]
                        total[k] = total[k] + jnp.sum(term.reshape(step // 8, 8, 128), 0)
        for k in range(count):
            dker[k : k + 1, lanes] = jnp.sum(total[k], 0, keepdims=True)


def tap_sum(xp, taps, out, flip):
    count = 31
    step = 128
    for q in range(0, out.shape[0], step):
        for c in range(xp.shape[1] // 128):
            lanes = slice(c * 128, (c + 1) * 128)
            window = xp[q : q + step + 32, lanes]
            total = jnp.zeros((step, 128), f32)
            for r in range(8):
                moved_by = shifted(window, r)
                for k in range(count):
                    if (k + 1) % 8 == r:
                        at = k + 1 - r
                        i = count - 1 - k if flip else k
                        total = total + taps[i : i + 1, lanes] * moved_by[at : at + step]
            out[q : q + step, lanes] = total


def to_rows(first, second):
    lane = lax.broadcasted_iota(jnp.int32, (128, 128), 1)
    return jnp.transpose(jnp.where(lane == 0, first, second))[:8]


def to_columns(first, second):
    row = lax.broadcasted_iota(jnp.int32, (128, 128), 0)
    return jnp.transpose(jnp.where(row == 0, first, second))


def k_front(
    where, taps, a0, a1, a2, a3, wab, ha, sg, xp, conv, stats, places,
    acts, heads, w, has, sgs, xps, convs, gated, spread, sems,
):
    s = where[0]
    rows = acts.shape[0] // N_SEQ
    part = has.shape[1]
    pieces = (a0, a1, a2, a3)
    loads = begin(
        sems, 9, [(a.at[pl.ds(rows, 16), pl.ds(0, 128)], heads.at[j]) for j, a in enumerate(pieces)]
    )
    weights = begin(sems, 4, [(wab, w)]) + begin(
        sems,
        0,
        [(a.at[pl.ds(0, rows)], acts.at[pl.ds(j * rows, rows)]) for j, a in enumerate(pieces)],
    )
    edge = jnp.zeros((16, part), f32)
    xps[0:16] = edge
    xps[16 + SPREAD :] = edge
    finish(loads)
    metas = [heads[j].astype(f32).astype(jnp.int32) for j in range(N_SEQ)]
    lens = [m[0:1, 0:1] for m in metas]
    bounds = [[m[0:1, i : i + 1] for i in range(1, 5)] for m in metas]
    offset = [
        n + GAP * sum((b < n).astype(jnp.int32) for b in bs) for n, bs in zip(lens, bounds)
    ]
    for j in range(N_SEQ):
        base = sum(((s ^ i) < (s ^ j)).astype(jnp.int32) * offset[i] for i in range(N_SEQ))
        o = lax.broadcasted_iota(jnp.int32, (8, rows), 1)
        label = sum((b <= o).astype(jnp.int32) for b in bounds[j])
        place = jnp.where(o < lens[j], base + o + GAP * label, -1)
        places[:, j * rows : (j + 1) * rows] = place.astype(f32)
    to_spread(places, spread)
    finish(weights)
    hidden = jnp.dot(acts[...], w[...], preferred_element_type=f32)
    gate = jax.nn.sigmoid(hidden[:, part:])
    has[...] = hidden[:, :part]
    sgs[...] = gate
    gated[...] = (hidden[:, :part] * gate).astype(bf16)
    stores = begin(sems, 5, [(has, ha), (sgs, sg)])
    xps[16 : 16 + SPREAD] = jnp.dot(spread[...], gated[...], preferred_element_type=f32)
    stores += begin(sems, 7, [(xps, xp)])
    tap_sum(xps, taps, convs, False)
    stores += begin(sems, 8, [(convs, conv)])
    for q in range(0, SPREAD, 128):
        x = convs[q : q + 128]
        mean = jnp.mean(x, 1, keepdims=True)
        square = jnp.sum((x - mean) * (x - mean), 1, keepdims=True)
        stats[:, q : q + 128] = to_rows(mean, square)
    finish(stores)


def load_grad_y(sems, pieces, out):
    rows = out.shape[0] // N_SEQ
    return begin(
        sems,
        0,
        [
            (p.at[pl.ds(rows + 16, rows)], out.at[pl.ds(j * rows, rows)])
            for j, p in enumerate(pieces)
        ],
    )


def k_mid(
    gain, stats, places, a0, a1, a2, a3, conv, swished, dwo, lines,
    gy, convs, swish, back, sw, dws, sems,
):
    part = convs.shape[1]
    width = part * N_SEQ
    first = begin(sems, 4, [(conv, convs)])
    loads = load_grad_y(sems, (a0, a1, a2, a3), gy)
    means = [stats[i, 0:1] for i in range(N_SEQ)]
    mean = sum(means) / N_SEQ
    square = sum(stats[i, 1:2] + part * (means[i] - mean) ** 2 for i in range(N_SEQ))
    inverse = lax.rsqrt(square / width + EPS)
    row = lax.broadcasted_iota(jnp.int32, (8, SPREAD), 0)
    lines[...] = jnp.where(row == 0, mean, inverse)
    to_back(places, back)
    finish(first)
    for q in range(0, SPREAD, 128):
        at = slice(q, q + 128)
        col = to_columns(mean[:, at], inverse[:, at])
        scaled = (convs[at] - col[:, 0:1]) * col[:, 1:2] * gain[...]
        swish[at] = (scaled * jax.nn.sigmoid(scaled)).astype(bf16)
    sw[...] = jnp.dot(back[...], swish[...], preferred_element_type=f32).astype(bf16)
    stores = begin(sems, 5, [(sw, swished)])
    finish(loads)
    rows = part // NY
    for i in range(NZ):
        term = column_product(sw[...], gy[:, i * part : (i + 1) * part])
        for j in range(NY):
            dws[i * NY + j] = term[j * rows : (j + 1) * rows].astype(bf16)
    stores += begin(sems, 6, [(dws, dwo)])
    finish(stores)


def k_grad(
    gain, lines, places, a0, a1, a2, a3, wo, conv, grad, stats, dgain,
    gy, w, convs, spread, grads, sems,
):
    part = convs.shape[1]
    loads = load_grad_y(sems, (a0, a1, a2, a3), gy)
    loads += begin(sems, 4, [(wo, w)])
    second = begin(sems, 5, [(conv, convs)])
    to_spread(places, spread)
    finish(loads)
    ds = jnp.zeros((gy.shape[0], part), f32)
    for i in range(NZ):
        at = slice(i * part, (i + 1) * part)
        ds = ds + row_product(gy[:, at], w[at])
    high = ds.astype(bf16)
    low = (ds - high.astype(f32)).astype(bf16)
    grads[...] = jnp.dot(spread[...], high, preferred_element_type=f32) + jnp.dot(
        spread[...], low, preferred_element_type=f32
    )
    finish(second)
    total = jnp.zeros((1, part), f32)
    for q in range(0, SPREAD, 128):
        at = slice(q, q + 128)
        col = to_columns(lines[0:1, at], lines[1:2, at])
        n = (convs[at] - col[:, 0:1]) * col[:, 1:2]
        scaled = n * gain[...]
        sig = jax.nn.sigmoid(scaled)
        d = grads[at] * sig * (1.0 + scaled * (1.0 - sig))
        total = total + jnp.sum(d * n, 0, keepdims=True)
        g = d * gain[...]
        grads[at] = g
        stats[:, at] = to_rows(
            jnp.sum(g, 1, keepdims=True), jnp.sum(g * n, 1, keepdims=True)
        )
    stores = begin(sems, 6, [(grads, grad)])
    dgain[...] = total
    finish(stores)


def k_back(
    stats, lines, places, taps, a0, a1, a2, a3, conv, grad, ha, sg, dconv, dab, dwi,
    convs, grads, acts, has, sgs, dp, dg, back, ds, dws, sems,
):
    part = convs.shape[1]
    width = part * N_SEQ
    rows = acts.shape[0] // N_SEQ
    loads = begin(sems, 0, [(conv, convs), (grad, grads)])
    gates = begin(sems, 2, [(ha, has), (sg, sgs)])
    later = begin(
        sems,
        4,
        [
            (a.at[pl.ds(0, rows)], acts.at[pl.ds(j * rows, rows)])
            for j, a in enumerate((a0, a1, a2, a3))
        ],
    )
    to_back(places, back)
    first = sum(stats[i, 0:1] for i in range(N_SEQ)) / width
    second = sum(stats[i, 1:2] for i in range(N_SEQ)) / width
    edge = jnp.zeros((16, part), f32)
    dp[0:16] = edge
    dp[16 + SPREAD :] = edge
    finish(loads)
    for q in range(0, SPREAD, 128):
        at = slice(q, q + 128)
        line = to_columns(lines[0:1, at], lines[1:2, at])
        col = to_columns(first[:, at], second[:, at])
        n = (convs[at] - line[:, 0:1]) * line[:, 1:2]
        dp[q + 16 : q + 144] = line[:, 1:2] * (grads[at] - col[:, 0:1] - n * col[:, 1:2])
    stores = begin(sems, 8, [(dp.at[pl.ds(16, SPREAD)], dconv)])
    tap_sum(dp, taps, dg, True)
    x = dg[...]
    high = x.astype(bf16)
    low = (x - high.astype(f32)).astype(bf16)
    finish(gates)
    d = jnp.dot(back[...], high, preferred_element_type=f32) + jnp.dot(
        back[...], low, preferred_element_type=f32
    )
    gate = sgs[...]
    ds[:, 0:part] = (d * gate).astype(bf16)
    ds[:, part:] = (d * has[...] * gate * (1.0 - gate)).astype(bf16)
    stores += begin(sems, 9, [(ds, dab)])
    finish(later)
    for i in range(N_SEQ):
        at = slice(i * part, (i + 1) * part)
        dws[at] = column_product(acts[:, at], ds[...]).astype(bf16)
        block = pl.ds(i * part, part)
        stores += begin(sems, 10 + i, [(dws.at[block], dwi.at[block])])
    finish(stores)


def k_dact(dab, wab, own, sent):
    rows = dab.shape[0] // N_SEQ
    term = row_product(dab[...], wab[...])
    for j in range(N_SEQ):
        out = own if j % 2 == 0 else sent
        out[j // 2] = term[j * rows : (j + 1) * rows].astype(out.dtype)


def k_proj(swished, wo, own, sent):
    rows = swished.shape[0] // N_SEQ
    part = swished.shape[1]
    for i in range(NZ):
        at = slice(i * part, (i + 1) * part)
        term = jnp.dot(swished[...], wo[at], preferred_element_type=f32)
        for j in range(N_SEQ):
            out = own if j % 2 == 0 else sent
            out[j // 2, :, at] = term[j * rows : (j + 1) * rows].astype(out.dtype)


def k_forward(own, core, sent):
    sent[...] = (own[1] + core[1].astype(f32)).astype(bf16)


def k_finish(meta, xs, gy, gain, own, core, far, grads, dgain):
    rows = xs.shape[0]
    x = xs[...].astype(f32)
    valid = lax.broadcasted_iota(jnp.int32, (rows, 1), 0) < meta[0]
    dact = own[0] + core[0].astype(f32) + far[...].astype(f32)
    normed, inverse = layer_norm(x)
    dgain[...] = jnp.sum(dact * normed, 0, keepdims=True)
    dx = norm_back(dact * gain[...], normed, inverse)
    grads[...] = jnp.where(valid, gy[rows + 16 :].astype(f32) + dx, 0.0).astype(bf16)


def k_outputs(meta, xs, own, core, far, outputs):
    rows = xs.shape[0]
    valid = lax.broadcasted_iota(jnp.int32, (rows, 1), 0) < meta[0]
    proj = own[0] + core[0].astype(f32) + far[...].astype(f32)
    outputs[...] = jnp.where(valid, xs[...].astype(f32) + proj, 0.0).astype(bf16)


def shards(frames, cotangent, gain_in, w_in, kernel, gain_mid, w_out, group_len, starts):
    taps_count = kernel.shape[0]
    rows, width = frames.shape[1:]
    part = width // N_SEQ
    s = lax.axis_index("seq")
    wide = lax.axis_index("wide")
    z, y, x = wide // (NY * NX), (wide // NX) % NY, wide % NX
    mine = s * part

    wab = jnp.concatenate(
        [
            lax.dynamic_slice_in_dim(w_in, mine, part, 1),
            lax.dynamic_slice_in_dim(w_in, width + mine, part, 1),
        ],
        1,
    )
    pair = to_all(wab, x)
    wo = swap_z_seq(lax.dynamic_slice_in_dim(w_out, mine, part, 1))
    xs = frames[0]

    meta = jnp.concatenate([group_len[0], starts[0]])
    gain_row = gain_in[None]
    (own_rows,) = local(
        k_norm,
        [((2 * rows + 16, width), bf16)],
        meta,
        xs,
        cotangent[0],
        gain_row,
        scalars=1,
    )
    wab = exchange(copies(pair)).reshape(width, 2 * part)
    pieces = gather_seq(own_rows)
    taps = lax.dynamic_slice_in_dim(kernel, mine, part, 1)
    gain = lax.dynamic_slice_in_dim(gain_mid, mine, part, 0)[None]
    slots = N_SEQ * rows
    wide_f32, slot_f32 = ((SPREAD, part), f32), ((slots, part), f32)
    rows_f32, padded_f32 = ((8, SPREAD), f32, True), ((SPREAD + 32, part), f32)
    hot, hot_back = ((SPREAD, slots), bf16), ((slots, SPREAD), bf16)
    all_rows, slot_bf16 = ((slots, width), bf16), ((slots, part), bf16)
    ha, sg, xp, conv, stats, places = manual(
        k_front,
        [slot_f32, slot_f32, padded_f32, wide_f32, rows_f32, ((8, slots), f32, True)],
        s[None],
        taps,
        *pieces,
        wab,
        scalars=1,
        fast=1,
        scratch=[
            all_rows,
            ((N_SEQ, 16, 128), bf16),
            ((width, 2 * part), bf16),
            slot_f32,
            slot_f32,
            padded_f32,
            wide_f32,
            slot_bf16,
            hot,
        ],
        sems=13,
    )
    wo = after(wo, wab)
    neighbour = after(swap_wide(wo, "x", 1), stats)
    wo = copies(jnp.concatenate(in_order([wo, neighbour], x), 0)[None])
    wo = exchange(wo).reshape(width, part)
    stats = lax.all_gather(stats, "seq")
    blocks = ((NZ * NY, part // NY, part), bf16)
    swished, dwo, lines = manual(
        k_mid,
        [slot_bf16, blocks, rows_f32],
        gain,
        stats,
        places,
        *pieces,
        conv,
        fast=3,
        scratch=[all_rows, wide_f32, ((SPREAD, part), bf16), hot_back, slot_bf16, blocks],
        sems=7,
    )
    dwo = from_all(after(dwo, wo))
    grad, stats, dgain_mid = manual(
        k_grad,
        [wide_f32, rows_f32, ((1, part), f32, True)],
        gain,
        lines,
        places,
        *pieces,
        wo,
        conv,
        fast=3,
        scratch=[all_rows, ((width, part), bf16), wide_f32, hot, wide_f32],
        sems=7,
    )
    stats = lax.all_gather(stats, "seq")
    both, weights = ((slots, 2 * part), bf16), ((width, 2 * part), bf16)
    dconv, dab, dwab = manual(
        k_back,
        [wide_f32, both, weights],
        stats,
        lines,
        places,
        taps,
        *pieces,
        conv,
        grad,
        ha,
        sg,
        fast=4,
        scratch=[
            wide_f32,
            wide_f32,
            all_rows,
            slot_f32,
            slot_f32,
            padded_f32,
            wide_f32,
            hot_back,
            both,
            weights,
        ],
        sems=14,
    )
    dwab = after(dwab.reshape(NZ * NY, -1, 2 * part), dwo)
    dab, swished, dconv = lax.optimization_barrier((dab, swished, dconv, dwab))[:3]
    dwab = from_all(dwab)

    halves = [((2, rows, width), f32), ((2, rows, width), bf16)]
    own, sent = local(k_dact, halves, dab, wab)
    core = swap_seq(sent, 1)
    dwo = own_half(dwo, x)
    own2, sent2 = local(k_proj, halves, after(swished, sent), wo)
    core2 = swap_seq(sent2, 1)
    (sent,) = local(k_forward, [((rows, width), bf16)], own, core)
    far = swap_seq(sent, 2)
    (sent2,) = local(k_forward, [((rows, width), bf16)], own2, core2)
    far2 = swap_seq(sent2, 2)
    (dker,) = local(k_taps, [((taps_count, part), f32)], after(dconv, sent2), xp)
    own = after(own, dker)
    grad_frames, dgain_in = local(
        k_finish,
        [((rows, width), bf16), ((1, width), f32)],
        meta,
        xs,
        own_rows,
        gain_row,
        own,
        core,
        far,
        scalars=1,
    )
    (outputs,) = local(
        k_outputs, [((rows, width), bf16)], meta, xs, own2, core2, far2, scalars=1
    )
    small = jnp.concatenate([dker, dgain_mid, dgain_in.reshape(N_SEQ, part)], 0)
    small = small + swap_wide(small, "x", 1)
    dwo = swap_z_seq(after(dwo, dwab))
    dwab = own_half(dwab, x)
    for axis in ("z", "y"):
        if axis == "y":
            small = after(small, dwab)
        small = (small + swap_wide(small, axis, 1)) + (
            swap_wide(small, axis, 2) + swap_wide(small, axis, 3)
        )
    small = [small] + [swap_seq(small, d) for d in (1, 2, 3)]
    total = (small[0] + small[1]) + (small[2] + small[3])
    grad_gain_in = total[taps_count + 1 :].reshape(width)
    small = in_order([a[: taps_count + 1] for a in small], s)
    small = jnp.concatenate(small, 1)
    grad_kernel = small[:taps_count]
    grad_gain_mid = small[taps_count]

    share = jnp.concatenate([dwab, dwo], 1)
    share = in_order([share] + [swap_seq(share, d) for d in (1, 2, 3)], s)
    grad_w_in = jnp.concatenate(
        [a[:, :part] for a in share] + [a[:, part : 2 * part] for a in share], 1
    ).astype(f32)
    grad_w_out = jnp.concatenate([a[:, 2 * part :] for a in share], 1).astype(f32)
    return (
        outputs[None],
        grad_frames[None],
        grad_w_in,
        grad_w_out,
        grad_kernel,
        grad_gain_in,
        grad_gain_mid,
    )


def solution(mesh):
    return jax.shard_map(
        shards,
        mesh=mesh,
        in_specs=(
            P("wide", "seq", None),
            P("wide", "seq", None),
            P(),
            P("wide", None),
            P(),
            P(),
            P("wide", None),
            P("wide", "seq"),
            P("wide", "seq"),
        ),
        out_specs=(
            P("wide", "seq", None),
            P("wide", "seq", None),
            P("wide", None),
            P("wide", None),
            P(),
            P(),
            P(),
        ),
        check_vma=False,
    )
```

```python
import jax
import jax.numpy as jnp
from jax import lax
from jax.experimental import pallas as pl
from jax.experimental.pallas import tpu as pltpu
from jax.sharding import PartitionSpec as P

EPS = 1e-05
N_SEQ = 4
NZ, NY, NX = 4, 4, 2
GAP = 16
SPREAD = 768
bf16 = jnp.bfloat16
f32 = jnp.float32


def wide_index(z, y, x):
    return (z * NY + y) * NX + x


def swap_seq(value, d):
    return lax.ppermute(value, "seq", [(i, i ^ d) for i in range(N_SEQ)])


def swap_wide(value, axis, d):
    pairs = []
    for z in range(NZ):
        for y in range(NY):
            for x in range(NX):
                to = {"z": (z ^ d, y, x), "y": (z, y ^ d, x), "x": (z, y, x ^ d)}[axis]
                pairs.append((wide_index(z, y, x), wide_index(*to)))
    return lax.ppermute(value, "wide", pairs)


def after(value, *others):
    return lax.optimization_barrier((value,) + others)[0]


def swap_z_seq(value):
    pairs = []
    for s in range(N_SEQ):
        for z in range(NZ):
            for y in range(NY):
                for x in range(NX):
                    pairs.append(
                        (s * 32 + wide_index(z, y, x), z * 32 + wide_index(s, y, x))
                    )
    return lax.ppermute(value, ("seq", "wide"), pairs)


def in_order(pieces, me):
    count = len(pieces)
    d = 1
    while d < count:
        odd = (me & d) != 0
        pieces = [jnp.where(odd, pieces[j ^ d], pieces[j]) for j in range(count)]
        d *= 2
    return pieces


PLANES = [[wide_index(z, y, x) for z in range(NZ) for y in range(NY)] for x in range(NX)]


def exchange(blocks):
    return lax.all_to_all(blocks, "wide", 0, 0, axis_index_groups=PLANES, tiled=True)


def to_all(block, x):
    pair = jnp.concatenate(in_order([block, swap_wide(block, "x", 1)], x), 0)
    return pair[None]


def copies(pair):
    return jnp.broadcast_to(pair, (NZ * NY,) + pair.shape[1:])


def from_all(blocks):
    return jnp.sum(exchange(blocks).astype(f32), 0)


def own_half(rows, x):
    pair = rows.reshape(NX, rows.shape[0] // NX, rows.shape[1])
    sent = lax.dynamic_index_in_dim(pair, x ^ 1, 0, False).astype(bf16)
    own = lax.dynamic_index_in_dim(pair, x, 0, False)
    return (own + swap_wide(sent, "x", 1).astype(f32)).astype(bf16)


def gather_seq(value):
    far = swap_seq(value, 2)
    return [value, swap_seq(value, 1), far, swap_seq(far, 1)]


def layer_norm(values):
    mean = jnp.mean(values, -1, keepdims=True)
    centred = values - mean
    inverse = lax.rsqrt(jnp.mean(centred * centred, -1, keepdims=True) + EPS)
    return (centred * inverse, inverse)


def norm_back(grad, normed, inverse):
    return inverse * (
        grad
        - jnp.mean(grad, -1, keepdims=True)
        - normed * jnp.mean(grad * normed, -1, keepdims=True)
    )


def column_product(left, right):
    return lax.dot_general(left, right, (((0,), (0,)), ((), ())), preferred_element_type=f32)


def row_product(left, right):
    return lax.dot_general(left, right, (((1,), (1,)), ((), ())), preferred_element_type=f32)


def local(body, outs, *args, scalars=0, scratch=(), sems=0, cost=(0, 0)):
    place = pl.BlockSpec(memory_space=pl.ANY if sems else pltpu.VMEM)
    specs = [pl.BlockSpec(memory_space=pltpu.SMEM)] * scalars
    specs += [place] * (len(args) - scalars)
    return pl.pallas_call(
        body,
        out_shape=[jax.ShapeDtypeStruct(shape, kind) for shape, kind in outs],
        in_specs=specs,
        out_specs=[place] * len(outs),
        scratch_shapes=[pltpu.VMEM(shape, kind) for shape, kind in scratch]
        + [pltpu.SemaphoreType.DMA((sems,))] * (sems > 0),
        compiler_params=pltpu.CompilerParams(vmem_limit_bytes=14 * 1024 * 1024),
        cost_estimate=pl.CostEstimate(
            flops=cost[0], bytes_accessed=cost[1], transcendentals=0
        ),
        name=body.__name__,
    )(*args)


def k_norm(meta, xs, cot, gain, out):
    rows, width = xs.shape
    normed, _ = layer_norm(xs[...].astype(f32))
    out[:rows] = (normed * gain[...]).astype(bf16)
    lane = lax.broadcasted_iota(jnp.int32, (16, width), 1)
    extra = jnp.zeros((16, width), f32)
    for i in range(meta.shape[0]):
        extra = jnp.where(lane == i, meta[i].astype(f32), extra)
    out[rows : rows + 16] = extra.astype(bf16)
    row = lax.broadcasted_iota(jnp.int32, (rows, width), 0)
    out[rows + 16 :] = jnp.where(row < meta[0], cot[...].astype(f32), 0.0).astype(bf16)


def manual(body, outs, *args, scalars=0, fast=0, scratch=(), sems=0):
    vmem = pl.BlockSpec(memory_space=pltpu.VMEM)
    large = pl.BlockSpec(memory_space=pl.ANY)
    specs = [pl.BlockSpec(memory_space=pltpu.SMEM)] * scalars + [vmem] * fast
    specs += [large] * (len(args) - scalars - fast)
    return pl.pallas_call(
        body,
        out_shape=[jax.ShapeDtypeStruct(o[0], o[1]) for o in outs],
        in_specs=specs,
        out_specs=[vmem if len(o) > 2 else large for o in outs],
        scratch_shapes=[pltpu.VMEM(shape, kind) for shape, kind in scratch]
        + [pltpu.SemaphoreType.DMA((sems,))],
        compiler_params=pltpu.CompilerParams(vmem_limit_bytes=60 * 1024 * 1024),
        cost_estimate=pl.CostEstimate(flops=0, bytes_accessed=0, transcendentals=0),
        name=body.__name__,
    )(*args)


def begin(sems, first, pairs):
    copies = [
        pltpu.make_async_copy(a, b, sems.at[first + i]) for i, (a, b) in enumerate(pairs)
    ]
    for c in copies:
        c.start()
    return copies


def finish(copies):
    for c in copies:
        c.wait()


def to_spread(places, out):
    for j in range(out.shape[1] // 128):
        at = slice(j * 128, (j + 1) * 128)
        spots = lax.broadcasted_iota(jnp.int32, (out.shape[0], 128), 0).astype(f32)
        out[:, at] = jnp.where(spots == places[0:1, at], 1.0, 0.0).astype(bf16)


def to_back(places, out):
    for j in range(out.shape[0] // 128):
        at = slice(j * 128, (j + 1) * 128)
        column = jnp.transpose(jnp.broadcast_to(places[0:1, at], (128, 128)))[:, 0:1]
        spots = lax.broadcasted_iota(jnp.int32, (128, out.shape[1]), 1).astype(f32)
        out[at] = jnp.where(spots == column, 1.0, 0.0).astype(bf16)


def shifted(x, r):
    return x if r == 0 else pltpu.roll(x, x.shape[0] - r, 0)


def k_taps(dconv, xp, dker):
    count = 31
    step = 128
    for c in range(dconv.shape[1] // 128):
        lanes = slice(c * 128, (c + 1) * 128)
        total = [jnp.zeros((8, 128), f32)] * count
        for q in range(0, dconv.shape[0], step):
            d = dconv[q : q + step, lanes]
            window = xp[q : q + step + 32, lanes]
            for r in range(8):
                moved_by = shifted(window, r)
                for k in range(count):
                    if (k + 1) % 8 == r:
                        at = k + 1 - r
                        term = d * moved_by[at : at + step]
                        total[k] = total[k] + jnp.sum(term.reshape(step // 8, 8, 128), 0)
        for k in range(count):
            dker[k : k + 1, lanes] = jnp.sum(total[k], 0, keepdims=True)


def tap_sum(xp, taps, out, flip):
    count = 31
    step = 128
    for q in range(0, out.shape[0], step):
        for c in range(xp.shape[1] // 128):
            lanes = slice(c * 128, (c + 1) * 128)
            window = xp[q : q + step + 32, lanes]
            total = jnp.zeros((step, 128), f32)
            for r in range(8):
                moved_by = shifted(window, r)
                for k in range(count):
                    if (k + 1) % 8 == r:
                        at = k + 1 - r
                        i = count - 1 - k if flip else k
                        total = total + taps[i : i + 1, lanes] * moved_by[at : at + step]
            out[q : q + step, lanes] = total


def to_rows(first, second):
    lane = lax.broadcasted_iota(jnp.int32, (128, 128), 1)
    return jnp.transpose(jnp.where(lane == 0, first, second))[:2]


def to_columns(first, second):
    row = lax.broadcasted_iota(jnp.int32, (128, 128), 0)
    return jnp.transpose(jnp.where(row == 0, first, second))


def k_front(
    where, taps, a0, a1, a2, a3, wab, ha, sg, xp, conv, stats, places,
    acts, heads, w, has, sgs, xps, convs, gated, spread, sems,
):
    s = where[0]
    rows = acts.shape[0] // N_SEQ
    part = has.shape[1]
    pieces = (a0, a1, a2, a3)
    loads = begin(
        sems, 9, [(a.at[pl.ds(rows, 16), pl.ds(0, 128)], heads.at[j]) for j, a in enumerate(pieces)]
    )
    weights = begin(sems, 4, [(wab, w)]) + begin(
        sems,
        0,
        [(a.at[pl.ds(0, rows)], acts.at[pl.ds(j * rows, rows)]) for j, a in enumerate(pieces)],
    )
    edge = jnp.zeros((16, part), f32)
    xps[0:16] = edge
    xps[16 + SPREAD :] = edge
    finish(loads)
    metas = [heads[j].astype(f32).astype(jnp.int32) for j in range(N_SEQ)]
    lens = [m[0:1, 0:1] for m in metas]
    bounds = [[m[0:1, i : i + 1] for i in range(1, 5)] for m in metas]
    offset = [
        n + GAP * sum((b < n).astype(jnp.int32) for b in bs) for n, bs in zip(lens, bounds)
    ]
    for j in range(N_SEQ):
        base = sum(((s ^ i) < (s ^ j)).astype(jnp.int32) * offset[i] for i in range(N_SEQ))
        o = lax.broadcasted_iota(jnp.int32, (8, rows), 1)
        label = sum((b <= o).astype(jnp.int32) for b in bounds[j])
        place = jnp.where(o < lens[j], base + o + GAP * label, -1)
        places[:, j * rows : (j + 1) * rows] = place.astype(f32)
    to_spread(places, spread)
    finish(weights)
    hidden = jnp.dot(acts[...], w[...], preferred_element_type=f32)
    gate = jax.nn.sigmoid(hidden[:, part:])
    has[...] = hidden[:, :part]
    sgs[...] = gate
    gated[...] = (hidden[:, :part] * gate).astype(bf16)
    stores = begin(sems, 5, [(has, ha), (sgs, sg)])
    xps[16 : 16 + SPREAD] = jnp.dot(spread[...], gated[...], preferred_element_type=f32)
    stores += begin(sems, 7, [(xps, xp)])
    tap_sum(xps, taps, convs, False)
    stores += begin(sems, 8, [(convs, conv)])
    for q in range(0, SPREAD, 128):
        x = convs[q : q + 128]
        mean = jnp.mean(x, 1, keepdims=True)
        square = jnp.sum((x - mean) * (x - mean), 1, keepdims=True)
        stats[:, q : q + 128] = to_rows(mean, square)
    finish(stores)


def load_grad_y(sems, pieces, out):
    rows = out.shape[0] // N_SEQ
    return begin(
        sems,
        0,
        [
            (p.at[pl.ds(rows + 16, rows)], out.at[pl.ds(j * rows, rows)])
            for j, p in enumerate(pieces)
        ],
    )


def k_mid(
    gain, stats, places, a0, a1, a2, a3, conv, swished, dwo, lines,
    gy, convs, swish, back, sw, dws, sems,
):
    part = convs.shape[1]
    width = part * N_SEQ
    first = begin(sems, 4, [(conv, convs)])
    loads = load_grad_y(sems, (a0, a1, a2, a3), gy)
    means = [stats[i, 0:1] for i in range(N_SEQ)]
    mean = sum(means) / N_SEQ
    square = sum(stats[i, 1:2] + part * (means[i] - mean) ** 2 for i in range(N_SEQ))
    inverse = lax.rsqrt(square / width + EPS)
    row = lax.broadcasted_iota(jnp.int32, (8, SPREAD), 0)
    lines[...] = jnp.where(row == 0, mean, inverse)
    to_back(places, back)
    finish(first)
    for q in range(0, SPREAD, 128):
        at = slice(q, q + 128)
        col = to_columns(mean[:, at], inverse[:, at])
        scaled = (convs[at] - col[:, 0:1]) * col[:, 1:2] * gain[...]
        swish[at] = (scaled * jax.nn.sigmoid(scaled)).astype(bf16)
    sw[...] = jnp.dot(back[...], swish[...], preferred_element_type=f32).astype(bf16)
    stores = begin(sems, 5, [(sw, swished)])
    finish(loads)
    rows = part // NY
    for i in range(NZ):
        term = column_product(sw[...], gy[:, i * part : (i + 1) * part])
        for j in range(NY):
            dws[i * NY + j] = term[j * rows : (j + 1) * rows].astype(bf16)
    stores += begin(sems, 6, [(dws, dwo)])
    finish(stores)


def k_grad(
    gain, lines, places, a0, a1, a2, a3, wo, conv, grad, stats, dgain,
    gy, w, convs, spread, grads, sems,
):
    part = convs.shape[1]
    loads = load_grad_y(sems, (a0, a1, a2, a3), gy)
    loads += begin(sems, 4, [(wo, w)])
    second = begin(sems, 5, [(conv, convs)])
    to_spread(places, spread)
    finish(loads)
    ds = jnp.zeros((gy.shape[0], part), f32)
    for i in range(NZ):
        at = slice(i * part, (i + 1) * part)
        ds = ds + row_product(gy[:, at], w[at])
    high = ds.astype(bf16)
    low = (ds - high.astype(f32)).astype(bf16)
    grads[...] = jnp.dot(spread[...], high, preferred_element_type=f32) + jnp.dot(
        spread[...], low, preferred_element_type=f32
    )
    finish(second)
    total = jnp.zeros((1, part), f32)
    for q in range(0, SPREAD, 128):
        at = slice(q, q + 128)
        col = to_columns(lines[0:1, at], lines[1:2, at])
        n = (convs[at] - col[:, 0:1]) * col[:, 1:2]
        scaled = n * gain[...]
        sig = jax.nn.sigmoid(scaled)
        d = grads[at] * sig * (1.0 + scaled * (1.0 - sig))
        total = total + jnp.sum(d * n, 0, keepdims=True)
        g = d * gain[...]
        grads[at] = g
        stats[:, at] = to_rows(
            jnp.sum(g, 1, keepdims=True), jnp.sum(g * n, 1, keepdims=True)
        )
    stores = begin(sems, 6, [(grads, grad)])
    dgain[...] = total
    finish(stores)


def k_back(
    stats, lines, places, taps, a0, a1, a2, a3, conv, grad, ha, sg, dconv, dab, dwi,
    convs, grads, acts, has, sgs, dp, dg, back, ds, dws, sems,
):
    part = convs.shape[1]
    width = part * N_SEQ
    rows = acts.shape[0] // N_SEQ
    loads = begin(sems, 0, [(conv, convs), (grad, grads)])
    gates = begin(sems, 2, [(ha, has), (sg, sgs)])
    later = begin(
        sems,
        4,
        [
            (a.at[pl.ds(0, rows)], acts.at[pl.ds(j * rows, rows)])
            for j, a in enumerate((a0, a1, a2, a3))
        ],
    )
    to_back(places, back)
    first = sum(stats[i, 0:1] for i in range(N_SEQ)) / width
    second = sum(stats[i, 1:2] for i in range(N_SEQ)) / width
    edge = jnp.zeros((16, part), f32)
    dp[0:16] = edge
    dp[16 + SPREAD :] = edge
    finish(loads)
    for q in range(0, SPREAD, 128):
        at = slice(q, q + 128)
        line = to_columns(lines[0:1, at], lines[1:2, at])
        col = to_columns(first[:, at], second[:, at])
        n = (convs[at] - line[:, 0:1]) * line[:, 1:2]
        dp[q + 16 : q + 144] = line[:, 1:2] * (grads[at] - col[:, 0:1] - n * col[:, 1:2])
    stores = begin(sems, 8, [(dp.at[pl.ds(16, SPREAD)], dconv)])
    tap_sum(dp, taps, dg, True)
    x = dg[...]
    high = x.astype(bf16)
    low = (x - high.astype(f32)).astype(bf16)
    finish(gates)
    d = jnp.dot(back[...], high, preferred_element_type=f32) + jnp.dot(
        back[...], low, preferred_element_type=f32
    )
    gate = sgs[...]
    ds[:, 0:part] = (d * gate).astype(bf16)
    ds[:, part:] = (d * has[...] * gate * (1.0 - gate)).astype(bf16)
    stores += begin(sems, 9, [(ds, dab)])
    finish(later)
    for i in range(N_SEQ):
        at = slice(i * part, (i + 1) * part)
        dws[at] = column_product(acts[:, at], ds[...]).astype(bf16)
        block = pl.ds(i * part, part)
        stores += begin(sems, 10 + i, [(dws.at[block], dwi.at[block])])
    finish(stores)


def k_dact(dab, wab, own, sent):
    rows = dab.shape[0] // N_SEQ
    term = row_product(dab[...], wab[...])
    for j in range(N_SEQ):
        out = own if j % 2 == 0 else sent
        out[j // 2] = term[j * rows : (j + 1) * rows].astype(out.dtype)


def k_proj(swished, wo, own, sent):
    rows = swished.shape[0] // N_SEQ
    part = swished.shape[1]
    for i in range(NZ):
        at = slice(i * part, (i + 1) * part)
        term = jnp.dot(swished[...], wo[at], preferred_element_type=f32)
        for j in range(N_SEQ):
            out = own if j % 2 == 0 else sent
            out[j // 2, :, at] = term[j * rows : (j + 1) * rows].astype(out.dtype)


def k_forward(own, core, sent):
    sent[...] = (own[1] + core[1].astype(f32)).astype(bf16)


def k_finish(meta, xs, gy, gain, own, core, far, grads, dgain):
    rows = xs.shape[0]
    x = xs[...].astype(f32)
    valid = lax.broadcasted_iota(jnp.int32, (rows, 1), 0) < meta[0]
    dact = own[0] + core[0].astype(f32) + far[...].astype(f32)
    normed, inverse = layer_norm(x)
    dgain[...] = jnp.sum(dact * normed, 0, keepdims=True)
    dx = norm_back(dact * gain[...], normed, inverse)
    grads[...] = jnp.where(valid, gy[rows + 16 :].astype(f32) + dx, 0.0).astype(bf16)


def k_outputs(meta, xs, own, core, far, outputs):
    rows = xs.shape[0]
    valid = lax.broadcasted_iota(jnp.int32, (rows, 1), 0) < meta[0]
    proj = own[0] + core[0].astype(f32) + far[...].astype(f32)
    outputs[...] = jnp.where(valid, xs[...].astype(f32) + proj, 0.0).astype(bf16)


def shards(frames, cotangent, gain_in, w_in, kernel, gain_mid, w_out, group_len, starts):
    taps_count = kernel.shape[0]
    rows, width = frames.shape[1:]
    part = width // N_SEQ
    s = lax.axis_index("seq")
    wide = lax.axis_index("wide")
    z, y, x = wide // (NY * NX), (wide // NX) % NY, wide % NX
    mine = s * part

    wab = jnp.concatenate(
        [
            lax.dynamic_slice_in_dim(w_in, mine, part, 1),
            lax.dynamic_slice_in_dim(w_in, width + mine, part, 1),
        ],
        1,
    )
    pair = to_all(wab, x)
    wo = swap_z_seq(lax.dynamic_slice_in_dim(w_out, mine, part, 1))
    xs = frames[0]

    meta = jnp.concatenate([group_len[0], starts[0]])
    gain_row = gain_in[None]
    (own_rows,) = local(
        k_norm,
        [((2 * rows + 16, width), bf16)],
        meta,
        xs,
        cotangent[0],
        gain_row,
        scalars=1,
    )
    wab = exchange(copies(pair)).reshape(width, 2 * part)
    pieces = gather_seq(own_rows)
    taps = lax.dynamic_slice_in_dim(kernel, mine, part, 1)
    gain = lax.dynamic_slice_in_dim(gain_mid, mine, part, 0)[None]
    slots = N_SEQ * rows
    wide_f32, slot_f32 = ((SPREAD, part), f32), ((slots, part), f32)
    rows_f32, padded_f32 = ((8, SPREAD), f32, True), ((SPREAD + 32, part), f32)
    two_rows = ((2, SPREAD), f32, True)
    hot, hot_back = ((SPREAD, slots), bf16), ((slots, SPREAD), bf16)
    all_rows, slot_bf16 = ((slots, width), bf16), ((slots, part), bf16)
    ha, sg, xp, conv, stats, places = manual(
        k_front,
        [slot_f32, slot_f32, padded_f32, wide_f32, two_rows, ((8, slots), f32, True)],
        s[None],
        taps,
        *pieces,
        wab,
        scalars=1,
        fast=1,
        scratch=[
            all_rows,
            ((N_SEQ, 16, 128), bf16),
            ((width, 2 * part), bf16),
            slot_f32,
            slot_f32,
            padded_f32,
            wide_f32,
            slot_bf16,
            hot,
        ],
        sems=13,
    )
    wo = after(wo, wab)
    neighbour = after(swap_wide(wo, "x", 1), stats)
    wo = copies(jnp.concatenate(in_order([wo, neighbour], x), 0)[None])
    wo = exchange(wo).reshape(width, part)
    stats = lax.all_gather(stats, "seq")
    blocks = ((NZ * NY, part // NY, part), bf16)
    swished, dwo, lines = manual(
        k_mid,
        [slot_bf16, blocks, rows_f32],
        gain,
        stats,
        places,
        *pieces,
        conv,
        fast=3,
        scratch=[all_rows, wide_f32, ((SPREAD, part), bf16), hot_back, slot_bf16, blocks],
        sems=7,
    )
    dwo = from_all(after(dwo, wo))
    grad, stats, dgain_mid = manual(
        k_grad,
        [wide_f32, two_rows, ((1, part), f32, True)],
        gain,
        lines,
        places,
        *pieces,
        wo,
        conv,
        fast=3,
        scratch=[all_rows, ((width, part), bf16), wide_f32, hot, wide_f32],
        sems=7,
    )
    stats = lax.all_gather(stats, "seq")
    both, weights = ((slots, 2 * part), bf16), ((width, 2 * part), bf16)
    dconv, dab, dwab = manual(
        k_back,
        [wide_f32, both, weights],
        stats,
        lines,
        places,
        taps,
        *pieces,
        conv,
        grad,
        ha,
        sg,
        fast=4,
        scratch=[
            wide_f32,
            wide_f32,
            all_rows,
            slot_f32,
            slot_f32,
            padded_f32,
            wide_f32,
            hot_back,
            both,
            weights,
        ],
        sems=14,
    )
    dwab = after(dwab.reshape(NZ * NY, -1, 2 * part), dwo)
    dab, swished, dconv = lax.optimization_barrier((dab, swished, dconv, dwab))[:3]
    dwab = from_all(dwab)

    halves = [((2, rows, width), f32), ((2, rows, width), bf16)]
    own, sent = local(k_dact, halves, dab, wab)
    core = swap_seq(sent, 1)
    dwo = own_half(dwo, x)
    own2, sent2 = local(k_proj, halves, after(swished, sent), wo)
    core2 = swap_seq(sent2, 1)
    (sent,) = local(k_forward, [((rows, width), bf16)], own, core)
    far = swap_seq(sent, 2)
    (sent2,) = local(k_forward, [((rows, width), bf16)], own2, core2)
    far2 = swap_seq(sent2, 2)
    (dker,) = local(k_taps, [((taps_count, part), f32)], after(dconv, sent2), xp)
    own = after(own, dker)
    grad_frames, dgain_in = local(
        k_finish,
        [((rows, width), bf16), ((1, width), f32)],
        meta,
        xs,
        own_rows,
        gain_row,
        own,
        core,
        far,
        scalars=1,
    )
    (outputs,) = local(
        k_outputs, [((rows, width), bf16)], meta, xs, own2, core2, far2, scalars=1
    )
    small = jnp.concatenate([dker, dgain_mid, dgain_in.reshape(N_SEQ, part)], 0)
    small = small + swap_wide(small, "x", 1)
    dwo = swap_z_seq(after(dwo, dwab))
    dwab = own_half(dwab, x)
    for axis in ("z", "y"):
        if axis == "y":
            small = after(small, dwab)
        small = (small + swap_wide(small, axis, 1)) + (
            swap_wide(small, axis, 2) + swap_wide(small, axis, 3)
        )
    small = [small] + [swap_seq(small, d) for d in (1, 2, 3)]
    total = (small[0] + small[1]) + (small[2] + small[3])
    grad_gain_in = total[taps_count + 1 :].reshape(width)
    small = in_order([a[: taps_count + 1] for a in small], s)
    small = jnp.concatenate(small, 1)
    grad_kernel = small[:taps_count]
    grad_gain_mid = small[taps_count]

    share = jnp.concatenate([dwab, dwo], 1)
    share = in_order([share] + [swap_seq(share, d) for d in (1, 2, 3)], s)
    grad_w_in = jnp.concatenate(
        [a[:, :part] for a in share] + [a[:, part : 2 * part] for a in share], 1
    ).astype(f32)
    grad_w_out = jnp.concatenate([a[:, 2 * part :] for a in share], 1).astype(f32)
    return (
        outputs[None],
        grad_frames[None],
        grad_w_in,
        grad_w_out,
        grad_kernel,
        grad_gain_in,
        grad_gain_mid,
    )


def solution(mesh):
    return jax.shard_map(
        shards,
        mesh=mesh,
        in_specs=(
            P("wide", "seq", None),
            P("wide", "seq", None),
            P(),
            P("wide", None),
            P(),
            P(),
            P("wide", None),
            P("wide", "seq"),
            P("wide", "seq"),
        ),
        out_specs=(
            P("wide", "seq", None),
            P("wide", "seq", None),
            P("wide", None),
            P("wide", None),
            P(),
            P(),
            P(),
        ),
        check_vma=False,
    )
```
